128 devices in a mesh: band: 32 (over y, z, core), sub: 4 (over x).
Axes of the slice: x: 4, y: 4, z: 4, core: 2. Of those that a mesh axis runs over, the one named last changes fastest.
Arguments:
- vorticity: float32 [8192, 8192], P(('band', 'sub')), may hold values from -6 to 6
Outputs:
- section_field: float32 [8192, 8192], P(('band', 'sub'))
- coarse_one: float32 [4096, 4096], P('band')
- coarse_two: float32 [2048, 2048], P('band')
The draws below stay inside these ranges and needn't reach their ends.
All inputs are finite; a program needn't handle non-finite values.
Results may differ from the reference program's by a relative error of at most 0.0001.
Values sent between devices are 32-bit elements; how exact they have to be, the bound alone decides.
A program may use at most 192 MiB of HBM per device.

```python
import math
import jax
import jax.numpy as jnp

N = 8192


def steps_of(stream_key, shape, split, smallest, top_value):
    def one(position, shards_of):
        draws = jax.random.uniform(jax.random.fold_in(jax.random.fold_in(stream_key, 6), position), (shards_of,), jnp.float32, smallest / len(split), top_value / len(split))
        return jnp.repeat(jnp.exp(draws), shape[position] // shards_of).reshape((-1,) + (1,) * (len(shape) - position - 1))

    factor_of = one(*split[0])
    for cut in split[1:]:
        factor_of = factor_of * one(*cut)
    return factor_of


def centred(key, shape, deviation, limit, pieces=(), held_as=jnp.bfloat16):
    level = steps_of(key, shape, pieces, -0.22, 0.18) if pieces else 1.0
    drawn = jax.random.normal(key, shape, jnp.float32) * deviation * level
    return jnp.minimum(jnp.maximum(drawn, -limit), limit).astype(held_as)


def setup_inputs(seed: int = 0) -> dict:
    streams_of = jax.random.split(jax.random.key(seed), 2)
    vorticity = centred(streams_of[0], (N, N), 1.0, 6.0, ((0, 128),), jnp.float32)
    return {"vorticity": vorticity}


time_step = 0.2
viscosity = 0.4
forcing = 1.0
force_waves = 4.0


def to_grid(spectrum, grid_size):
    return jnp.fft.irfft2(jnp.pad(spectrum, ((0, 0), (0, 1))), s=(grid_size, grid_size))


def reference(vorticity):
    length = vorticity.shape[0]
    half_len = length // 2
    cutoff = length // 3
    index_y = jnp.arange(length, dtype=jnp.int32)
    wave_y = jnp.where(index_y < half_len, index_y, index_y - length)
    wave_x = jnp.arange(half_len, dtype=jnp.int32)
    kept_modes = ((jnp.abs(wave_y)[:, None] <= cutoff) & (wave_x[None, :] <= cutoff)).astype(jnp.float32)
    factor = 2.0 * math.pi / length
    kappa_y = factor * wave_y.astype(jnp.float32)[:, None]
    kappa_x = factor * wave_x.astype(jnp.float32)[None, :]
    kappa_sq = kappa_x * kappa_x + kappa_y * kappa_y
    inverse_sq = jnp.where(kappa_sq > 0, 1.0 / jnp.where(kappa_sq > 0, kappa_sq, 1.0), 0.0)
    vort_hat = jnp.fft.rfft2(vorticity)[:, :half_len] * kept_modes
    stream = vort_hat * inverse_sq
    vel_x = to_grid(1j * kappa_y * stream, length)
    vel_y = to_grid(-1j * kappa_x * stream, length)
    grad_x = to_grid(1j * kappa_x * vort_hat, length)
    grad_y = to_grid(1j * kappa_y * vort_hat, length)
    positions = jnp.arange(length, dtype=jnp.int32).astype(jnp.float32)[:, None]
    drive_term = forcing * jnp.sin((2.0 * math.pi * force_waves / length) * positions)
    advect = vel_x * grad_x + vel_y * grad_y - drive_term
    adv_hat = jnp.fft.rfft2(advect)[:, :half_len] * kept_modes
    next_hat = vort_hat + (0.5 * time_step) * (-adv_hat - viscosity * kappa_sq * vort_hat)
    section_field = to_grid(next_hat, length)
    coarse_list = []
    for divisor in (2, 4):
        grid_size = length // divisor
        upper_half = grid_size // 2
        coarse_block = jnp.concatenate([next_hat[:upper_half, :upper_half], jnp.zeros((1, upper_half), next_hat.dtype), next_hat[length - upper_half + 1:, :upper_half]], axis=0)
        coarse_block = coarse_block * ((grid_size * grid_size) / (length * length))
        coarse_list.append(to_grid(coarse_block, grid_size))
    return section_field, coarse_list[0], coarse_list[1]
```

```python
import functools
import math

import jax
import jax.numpy as jnp
import ml_dtypes
import numpy as np
from jax import lax
from jax.experimental import pallas as pl
from jax.experimental.pallas import tpu as pltpu
from jax.sharding import PartitionSpec as P

time_step = 0.2
viscosity = 0.4
forcing = 1.0
force_waves = 4.0

N = 8192
CUT = N // 3
DEV = 128
AXES = ("band", "sub")
f32 = jnp.float32
bf16 = jnp.bfloat16


def halves(table):
    table = np.asarray(table, np.float64).astype(np.float32)
    high = table.astype(ml_dtypes.bfloat16)
    low = (table - high.astype(np.float32)).astype(ml_dtypes.bfloat16)
    return np.stack([high, low])


def wave_of(t):
    return np.where(t % 2 == 1, -(t + 1) // 2, t // 2)


def slot_index():
    e, i = np.meshgrid(np.arange(16), np.arange(11), indexing="ij")
    return e + 16 * i


def forward_row_tables():
    t = slot_index()
    p = np.arange(256)
    out = np.zeros((2, 16, 2, 12, 2, 256))
    ang = 2 * np.pi * ((wave_of(t)[:, :, None] * p) % 256) / 256
    out[0, :, 0, :11, 0], out[0, :, 0, :11, 1] = np.cos(ang), np.sin(ang)
    out[0, :, 1, :11, 0], out[0, :, 1, :11, 1] = -np.sin(ang), np.cos(ang)
    ang = 2 * np.pi * ((16 * t[:, :, None] * p) % N) / N
    odd = (t % 2 == 1)[:, :, None]
    out[1, :, 0, :11, 0], out[1, :, 1, :11, 0] = np.where(odd, 0, np.cos(ang)), np.where(odd, 0, -np.sin(ang))
    out[1, :, 0, :11, 1], out[1, :, 1, :11, 1] = np.where(odd, np.cos(ang), 0), np.where(odd, -np.sin(ang), 0)
    out *= (t <= 170)[None, :, None, :, None, None] if False else 1.0
    return halves(out[0].reshape(384, 512)), halves(out[1].reshape(384, 512))


def backward_row_values(t, length):
    plen = length // 32
    p = np.arange(plen)
    ang = 2 * np.pi * ((wave_of(t)[..., None] * p) % plen) / plen
    gen = np.zeros(t.shape + (2, 2, plen))
    gen[..., 0, 0, :], gen[..., 1, 0, :] = np.cos(ang), -np.sin(ang)
    gen[..., 0, 1, :], gen[..., 1, 1, :] = np.sin(ang), np.cos(ang)
    ang = 2 * np.pi * ((16 * t[..., None] * p) % length) / length
    odd = (t % 2 == 1)[..., None]
    spe = np.zeros(t.shape + (2, 2, plen))
    spe[..., 0, 0, :], spe[..., 1, 0, :] = np.where(odd, 0, np.cos(ang)), np.where(odd, 0, -np.sin(ang))
    spe[..., 0, 1, :], spe[..., 1, 1, :] = np.where(odd, np.cos(ang), 0), np.where(odd, -np.sin(ang), 0)
    return np.stack([gen, spe]).reshape((2,) + t.shape + (2, 2 * plen))


def backward_field_tables():
    v = backward_row_values(slot_index(), N)
    v = np.moveaxis(v, 3, 1).reshape(2, 352, 512)
    return halves(v[0]), halves(v[1])


def backward_next_tables():
    t = slot_index()
    v = backward_row_values(t, N)
    full = np.zeros((2, 16, 32, 512))
    for ri in range(2):
        full[:, :, ri * 11 : ri * 11 + 11] = v[:, :, :, ri]
    v1 = backward_row_values(t, N // 2)
    one = np.zeros((2, 2, 16, 32, 256))
    for ii in range(4):
        for ri in range(2):
            for ipar in range(2):
                one[:, ipar, :, 22 + 2 * ii + ri] = v1[:, :, 2 * ii + ipar, ri]
    v2 = backward_row_values(t, N // 4)
    two = np.zeros((2, 4, 16, 32, 128))
    for i in range(4):
        for ri in range(2):
            two[:, i, :, 30 + ri] = v2[:, :, i, ri]
    return (
        halves(full.reshape(2, 512, 512)),
        halves(one.reshape(2, 2, 512, 256)),
        halves(two.reshape(2, 4, 512, 128)),
    )


def row_twiddle(length):
    plen = length // 32
    ang = 2 * np.pi * np.arange(16)[:, None] * np.arange(plen) / length
    return (0.5 * np.stack([np.cos(ang), np.sin(ang)])).astype(np.float32)


def column_outer():
    ang = 2 * np.pi * ((np.arange(128)[:, None] * np.arange(128)) % 128) / 128
    c, s = np.cos(ang), np.sin(ang)
    return halves(np.block([[c, s], [-s, c]])), halves(np.block([[c, -s], [s, c]]))


def column_twiddle(rows_each, copies):
    length = DEV * rows_each
    ang = 2 * np.pi * np.arange(128)[:, None] * np.arange(rows_each) / length
    return np.stack([np.tile(np.cos(ang), (1, copies)), np.tile(np.sin(ang), (1, copies))]).astype(np.float32)


def column_inner(rows_each, copies, sign):
    j = np.arange(64)
    signed = np.where(j < 32, j, j - 64)
    ang = 2 * np.pi * ((signed[:, None] * np.arange(rows_each)) % rows_each) / rows_each
    keep = ((signed >= -rows_each // 2) & (signed < rows_each // 2))[:, None]
    c, s = np.cos(ang) * keep, np.sin(ang) * keep
    out = np.zeros((copies, 2, 2, 64, 2, copies, 2, rows_each))
    for m in range(copies):
        for k in range(2):
            out[m, 0, k, :, 0, m, k], out[m, 1, k, :, 0, m, k] = c, -s
            out[m, 0, k, :, 1, m, k], out[m, 1, k, :, 1, m, k] = s, c
    return out.reshape(copies * 256, 2 * copies * 2 * rows_each)


def cmul_const(a, ang):
    r, i = a
    n = round(ang / (math.pi / 16)) % 32
    if n == 0:
        return (r, i)
    if n == 8:
        return (-i, r)
    if n == 16:
        return (-r, -i)
    if n == 24:
        return (i, -r)
    h = math.sqrt(0.5)
    if n == 4:
        return ((r - i) * h, (r + i) * h)
    if n == 12:
        return ((r + i) * (-h), (r - i) * h)
    if n == 20:
        return ((i - r) * h, (r + i) * (-h))
    if n == 28:
        return ((r + i) * h, (i - r) * h)
    c, s = math.cos(n * math.pi / 16), math.sin(n * math.pi / 16)
    return (r * c - i * s, r * s + i * c)


def cadd(a, b):
    return (a[0] + b[0], a[1] + b[1])


def csub(a, b):
    return (a[0] - b[0], a[1] - b[1])


def fft_small(z, sign):
    n = len(z)
    if n == 1:
        return z
    if n == 2:
        return [cadd(z[0], z[1]), csub(z[0], z[1])]
    even, odd = fft_small(z[0::2], sign), fft_small(z[1::2], sign)
    out = [None] * n
    for k in range(n // 2):
        w = cmul_const(odd[k], sign * 2 * math.pi * k / n)
        out[k], out[k + n // 2] = cadd(even[k], w), csub(even[k], w)
    return out


def forward32(x):
    z = fft_small([(x[2 * m], x[2 * m + 1]) for m in range(16)], -1)
    ends = (z[0][0] + z[0][1], z[0][0] - z[0][1])
    rest = [None] * 16
    for k in range(1, 9):
        a, b = z[k], z[16 - k]
        even = (a[0] + b[0], a[1] - b[1])
        odd = (a[1] + b[1], b[0] - a[0])
        turned = cmul_const(odd, -2 * math.pi * k / 32)
        rest[k] = cadd(even, turned)
        if k < 8:
            other = csub(even, turned)
            rest[16 - k] = (other[0], -other[1])
    return ends, rest


def backward32(ends, rest):
    z = [None] * 16
    z[0] = (ends[0] + ends[1], ends[0] - ends[1])
    for k in range(1, 9):
        a, b = rest[k], rest[16 - k]
        even = (a[0] + b[0], a[1] - b[1])
        odd = cmul_const((a[0] - b[0], a[1] + b[1]), 2 * math.pi * k / 32)
        z[k] = (even[0] - odd[1], even[1] + odd[0])
        if k < 8:
            z[16 - k] = (even[0] + odd[1], odd[0] - even[1])
    z = fft_small(z, 1)
    out = []
    for m in range(16):
        out += [z[m][0], z[m][1]]
    return out


def split(x):
    high = x.astype(bf16)
    low = (x - high.astype(f32)).astype(bf16)
    return high, low


def mm(a, b, dims):
    return lax.dot_general(a, b, (dims, ((), ())), preferred_element_type=f32)


def dot_right(x, table, dims=((1,), (0,))):
    high, low = split(x)
    return mm(high, table[0], dims) + (mm(high, table[1], dims) + mm(low, table[0], dims))


def dot_left(table, x, dims=((1,), (0,))):
    high, low = split(x)
    return mm(table[0], high, dims) + (mm(table[0], low, dims) + mm(table[1], high, dims))


def pair(ref, *lead):
    return ref[(0,) + lead], ref[(1,) + lead]


def row_forward(x_ref, y_ref, tw_ref, fg_ref, fs_ref, put):
    def radix(step, _):
        rows = pl.ds(pl.multiple_of(step * 8, 8), 8)
        for h in range(2):
            lanes = pl.ds(128 * h, 128)
            x = [x_ref[rows, pl.ds(256 * q + 128 * h, 128)] for q in range(32)]
            ends, rest = forward32(x)
            y_ref[rows, pl.ds(128 * h, 128)] = ends[0]
            y_ref[rows, pl.ds(256 + 128 * h, 128)] = ends[1]
            for k in range(1, 16):
                c, s = tw_ref[0, k : k + 1, lanes], tw_ref[1, k : k + 1, lanes]
                r, i = rest[k]
                to = pl.ds(pl.multiple_of(k * 64 + step * 8, 8), 8)
                y_ref[to, pl.ds(128 * h, 128)] = r * c + i * s
                y_ref[to, pl.ds(256 + 128 * h, 128)] = i * c - r * s
        return 0

    lax.fori_loop(0, 8, radix, 0)

    def product(step, _):
        y = y_ref[pl.ds(pl.multiple_of(step * 256, 256), 256), :]
        out = dot_left(pair(fg_ref), y, ((1,), (1,)))
        put(2 * step, out[:, :128])
        put(2 * step + 1, out[:, 128:])
        return 0

    lax.fori_loop(0, 4, product, 0)
    return dot_left(pair(fs_ref), y_ref[:64, :], ((1,), (1,)))


def row_backward(get, u_ref, tw_ref, tables, special, rows_each, plen, finish):
    copies = 64 // rows_each

    def product(g, _):
        block = get(g)
        high, low = split(block)
        total = None
        hight, lowt = high.T, low.T
        for m in range(copies):
            part = slice(m * 2 * rows_each, (m + 1) * 2 * rows_each)
            th, tl = tables(m)
            one = mm(hight[part], th, ((1,), (0,))) + (mm(hight[part], tl, ((1,), (0,))) + mm(lowt[part], th, ((1,), (0,))))
            total = one if total is None else total + one
        u_ref[pl.ds(pl.multiple_of(g * 2 * rows_each, 2 * rows_each), 2 * rows_each), :] = total
        return 0

    lax.fori_loop(0, 8, product, 0)
    block = get(0)
    high, low = split(block)
    hight, lowt = high.T, low.T
    total = None
    for m in range(copies):
        part = slice(m * 2 * rows_each, (m + 1) * 2 * rows_each)
        th, tl = special(m)
        one = mm(hight[part], th, ((1,), (0,))) + (mm(hight[part], tl, ((1,), (0,))) + mm(lowt[part], th, ((1,), (0,))))
        total = one if total is None else total + one
    u_ref[:rows_each, :] = total[:rows_each]
    width = min(plen, 128)

    def radix(step, _):
        for h in range(plen // width):
            lanes = pl.ds(width * h, width)
            here = pl.ds(pl.multiple_of(step * 8, 8), 8)
            ends = (u_ref[here, lanes], u_ref[here, pl.ds(plen + width * h, width)])
            rest = [None] * 16
            for k in range(1, 16):
                c, s = tw_ref[0, k : k + 1, lanes], tw_ref[1, k : k + 1, lanes]
                at = pl.ds(pl.multiple_of(k * rows_each + step * 8, 8), 8)
                r, i = u_ref[at, lanes], u_ref[at, pl.ds(plen + width * h, width)]
                rest[k] = (r * c - i * s, r * s + i * c)
            finish(here, width * h, width, backward32(ends, rest))
        return 0

    lax.fori_loop(0, rows_each // 8, radix, 0)


def waves(me, i):
    g, e = me // 16, me % 16
    t = e + 16 * i
    lane = lax.broadcasted_iota(jnp.int32, (1, 128), 1)
    c = lane // 64
    k2 = 2 * g + c
    j2 = jnp.where(t % 2 == 1, -((t + 1) // 2), t // 2)
    kx = jnp.where(k2 == 0, 16 * t, k2 + 32 * j2)
    return kx


def wave_y():
    k = lax.broadcasted_iota(jnp.int32, (128, 128), 0)
    lane = lax.broadcasted_iota(jnp.int32, (128, 128), 1)
    j = lane % 64
    return k + 128 * jnp.where(j < 32, j, j - 64)


def column_forward(get, i, tc_ref, fo_ref, qf_ref):
    r = jnp.concatenate([get(i, 0), get(i, 1)], axis=0)
    out = dot_left(pair(fo_ref), r)
    r, im = out[:128], out[128:]
    c, s = tc_ref[0], tc_ref[1]
    turned = jnp.concatenate([r * c + im * s, im * c - r * s], axis=1)
    out = dot_right(turned, pair(qf_ref))
    return out[:, :128], out[:, 128:]


def column_backward(fields, tc_ref, bo_ref, qb_table):
    stacked = jnp.concatenate(fields, axis=0) if len(fields) > 1 else fields[0]
    u = dot_right(stacked, qb_table)
    c, s = tc_ref[0], tc_ref[1]
    cols = []
    for n in range(len(fields)):
        r, im = u[128 * n : 128 * n + 128, :128], u[128 * n : 128 * n + 128, 128:]
        cols.append(jnp.concatenate([r * c - im * s, r * s + im * c], axis=0))
    joined = jnp.concatenate(cols, axis=1) if len(cols) > 1 else cols[0]
    out = dot_left(pair(bo_ref), joined)
    return [out[:, 128 * n : 128 * n + 128] for n in range(len(fields))]


def spectral(me, i):
    kx = waves(me, i)
    ky = wave_y()
    kept = ((jnp.abs(kx) <= CUT) & (jnp.abs(ky) <= CUT)).astype(f32)
    factor = 2.0 * math.pi / N
    kappa_x, kappa_y = factor * kx.astype(f32), factor * ky.astype(f32)
    kappa_sq = kappa_x * kappa_x + kappa_y * kappa_y
    weight = jnp.where(kx == 0, 1.0, 2.0) / (float(N) * float(N))
    return kept, kappa_x, kappa_y, kappa_sq, weight, ky


def kernel_row_forward(x_ref, tw_ref, fg_ref, fs_ref, s_ref, y_ref):
    def put(g, value):
        s_ref[pl.ds(pl.multiple_of(g * 384, 384), 384), :] = value

    tail = row_forward(x_ref, y_ref, tw_ref, fg_ref, fs_ref, put)
    s_ref[:384, :64] = tail


def kernel_column_fields(r_ref, tc_ref, fo_ref, qf_ref, bo_ref, qb_ref, s_ref, vort_ref):
    me = lax.axis_index("band") * 4 + lax.axis_index("sub")

    def get(i, ri):
        return r_ref[pl.ds(ri * 12 + i, 128, stride=24), :]

    def slot(i, _):
        vr, vi = column_forward(get, i, tc_ref, fo_ref, qf_ref)
        kept, kappa_x, kappa_y, kappa_sq, weight, ky = spectral(me, i)
        vr, vi = vr * kept, vi * kept
        vort_ref[i, :, :128], vort_ref[i, :, 128:] = vr, vi
        positive = kappa_sq > 0
        inverse_sq = jnp.where(positive, 1.0 / jnp.where(positive, kappa_sq, 1.0), 0.0)
        sr, si = vr * inverse_sq, vi * inverse_sq
        kxw, kyw = kappa_x * weight, kappa_y * weight
        fields = [
            jnp.concatenate([-kyw * si, kyw * sr], axis=1),
            jnp.concatenate([kxw * si, -kxw * sr], axis=1),
            jnp.concatenate([-kxw * vi, kxw * vr], axis=1),
            jnp.concatenate([-kyw * vi, kyw * vr], axis=1),
        ]
        outs = column_backward(fields, tc_ref, bo_ref, pair(qb_ref))
        for f in range(4):
            for ri in range(2):
                s_ref[pl.ds(i * 8 + f * 2 + ri, 128, stride=88), :] = outs[f][128 * ri : 128 * ri + 128]
        return 0

    lax.fori_loop(0, 11, slot, 0)


def kernel_row_product(r_ref, tw_ref, gg_ref, gs_ref, fg_ref, fs_ref, s_ref, u_ref, a_ref, b_ref):
    me = lax.axis_index("band") * 4 + lax.axis_index("sub")

    def getter(f):
        def get(g):
            parts = [r_ref[pl.ds(g * 1408 + f * 2 + ri, 176, stride=8), :] for ri in range(2)]
            return jnp.concatenate(parts, axis=0)

        return get

    def keep(to):
        def finish(here, start, width, out):
            for q in range(32):
                to[here, pl.ds(256 * q + start, width)] = out[q]

        return finish

    def times(to):
        def finish(here, start, width, out):
            for q in range(32):
                at = pl.ds(256 * q + start, width)
                to[here, at] = to[here, at] * out[q]

        return finish

    def last(here, start, width, out):
        row = lax.broadcasted_iota(jnp.int32, (8, 128), 0) + (me * 64 + here.start)
        drive = forcing * jnp.sin((2.0 * math.pi * force_waves / N) * row.astype(f32))
        for q in range(32):
            at = pl.ds(256 * q + start, width)
            a_ref[here, at] = a_ref[here, at] + (b_ref[here, at] * out[q] - drive)

    tables, special = (lambda m: pair(gg_ref)), (lambda m: pair(gs_ref))
    for f, finish in ((0, keep(a_ref)), (2, times(a_ref)), (1, keep(b_ref)), (3, last)):
        row_backward(getter(f), u_ref, tw_ref, tables, special, 64, 256, finish)

    def put(g, value):
        s_ref[pl.ds(pl.multiple_of(g * 384, 384), 384), :] = value

    tail = row_forward(a_ref, u_ref, tw_ref, fg_ref, fs_ref, put)
    s_ref[:384, :64] = tail


def kernel_column_next(r_ref, vort_ref, tc_ref, tc1_ref, tc2_ref, fo_ref, qf_ref, bo_ref, qb_ref, q1_ref, q2_ref, s_ref, n_ref):
    me = lax.axis_index("band") * 4 + lax.axis_index("sub")

    def get(i, ri):
        return r_ref[pl.ds(ri * 12 + i, 128, stride=24), :]

    half_step = 0.5 * time_step

    def slot(i, _):
        ar, ai = column_forward(get, i, tc_ref, fo_ref, qf_ref)
        kept, kappa_x, kappa_y, kappa_sq, weight, ky = spectral(me, i)
        vr, vi = vort_ref[i, :, :128], vort_ref[i, :, 128:]
        ar, ai = ar * kept, ai * kept
        nr = (vr + half_step * (-ar - viscosity * kappa_sq * vr)) * weight
        ni = (vi + half_step * (-ai - viscosity * kappa_sq * vi)) * weight
        both = jnp.concatenate([nr, ni], axis=1)
        (out,) = column_backward([both], tc_ref, bo_ref, pair(qb_ref))
        for ri in range(2):
            s_ref[pl.ds(i + 11 * ri, 128, stride=32), :] = out[128 * ri : 128 * ri + 128]
        n_ref[i] = both
        return 0

    lax.fori_loop(0, 11, slot, 0)
    ky = wave_y()
    inside_one = jnp.concatenate([(jnp.abs(ky) < 2048).astype(f32)] * 2, axis=1)
    inside_two = jnp.concatenate([(jnp.abs(ky) < 1024).astype(f32)] * 2, axis=1)

    def first(m, _):
        block = jnp.concatenate([n_ref[2 * m] * inside_one, n_ref[2 * m + 1] * inside_one], axis=1)
        (out,) = column_backward([block], tc1_ref, bo_ref, pair(q1_ref))
        for ri in range(2):
            s_ref[pl.ds(22 + 2 * m + ri, 128, stride=32), :] = out[128 * ri : 128 * ri + 128]
        return 0

    lax.fori_loop(0, 4, first, 0)
    block = jnp.concatenate([n_ref[m] * inside_two for m in range(4)], axis=1)
    (out,) = column_backward([block], tc2_ref, bo_ref, pair(q2_ref))
    for ri in range(2):
        s_ref[pl.ds(30 + ri, 128, stride=32), :] = out[128 * ri : 128 * ri + 128]


def kernel_row_section(r_ref, tw_ref, g_ref, out_ref, u_ref):
    def get(g):
        return r_ref[pl.ds(pl.multiple_of(g * 512, 512), 512), :]

    def finish(here, start, width, out):
        for q in range(32):
            out_ref[here, pl.ds(256 * q + start, width)] = out[q]

    row_backward(get, u_ref, tw_ref, lambda m: pair(g_ref, 0), lambda m: pair(g_ref, 1), 64, 256, finish)


def kernel_row_coarse(r_ref, tw1_ref, tw2_ref, g1_ref, g2_ref, one_ref, two_ref, u1_ref, u2_ref):
    def get(g):
        return r_ref[pl.ds(pl.multiple_of(g * 512, 512), 512), :]

    def finish_one(here, start, width, out):
        for q in range(32):
            one_ref[here, pl.ds(128 * q + start, width)] = out[q]

    def finish_two(here, start, width, out):
        for q in range(16):
            two_ref[here, pl.ds(128 * q, 128)] = jnp.concatenate([out[2 * q], out[2 * q + 1]], axis=1)

    row_backward(get, u1_ref, tw1_ref, lambda m: pair(g1_ref, 0, m), lambda m: pair(g1_ref, 1, m), 32, 128, finish_one)
    row_backward(get, u2_ref, tw2_ref, lambda m: pair(g2_ref, 0, m), lambda m: pair(g2_ref, 1, m), 16, 64, finish_two)


def call(kernel, args, outs, scratch):
    vm = pl.BlockSpec(memory_space=pltpu.VMEM)
    shapes = [jax.ShapeDtypeStruct(s, f32) for s in outs]
    return pl.pallas_call(
        kernel,
        out_shape=shapes,
        in_specs=[vm] * len(args),
        out_specs=[vm] * len(outs),
        scratch_shapes=[pltpu.VMEM(s, f32) for s in scratch],
        compiler_params=pltpu.CompilerParams(vmem_limit_bytes=56 * 2**20),
    )(*args)


def exchange(x):
    rows = x.shape[0] // DEV
    out = lax.all_to_all(x.reshape(DEV, rows, 128), AXES, split_axis=0, concat_axis=0, tiled=True)
    return out.reshape(DEV * rows, 128)


def local(vorticity):
    fg, fs = forward_row_tables()
    gg, gs = backward_field_tables()
    g_full, g_one, g_two = backward_next_tables()
    tw, tw1, tw2 = row_twiddle(N), row_twiddle(N // 2), row_twiddle(N // 4)
    fo, bo = column_outer()
    tc, tc1, tc2 = column_twiddle(64, 2), column_twiddle(32, 4), column_twiddle(16, 8)
    inner = column_inner(64, 1, 1)
    qb, qf = halves(inner), halves(inner.T)
    q1, q2 = halves(column_inner(32, 2, 1)), halves(column_inner(16, 4, 1))

    (s1,) = call(kernel_row_forward, (vorticity, tw, fg, fs), [(3072, 128)], [(1024, 512)])
    r1 = exchange(s1)
    s2, vort = call(kernel_column_fields, (r1, tc, fo, qf, bo, qb), [(88 * 128, 128), (11, 128, 256)], [])
    r2 = exchange(s2)
    (s3,) = call(
        kernel_row_product,
        (r2, tw, gg, gs, fg, fs),
        [(3072, 128)],
        [(1024, 512), (64, N), (64, N)],
    )
    r3 = exchange(s3)
    (s4,) = call(
        kernel_column_next,
        (r3, vort, tc, tc1, tc2, fo, qf, bo, qb, q1, q2),
        [(32 * 128, 128)],
        [(11, 128, 256)],
    )
    r4 = exchange(s4)
    one, two = call(
        kernel_row_coarse, (r4, tw1, tw2, g_one, g_two), [(32, N // 2), (16, N // 4)], [(512, 256), (256, 128)]
    )
    coarse_one = lax.all_gather(one, "sub", axis=0, tiled=True)
    coarse_two = lax.all_gather(two, "sub", axis=0, tiled=True)
    (section,) = call(kernel_row_section, (r4, tw, g_full), [(64, N)], [(1024, 512)])
    return section, coarse_one, coarse_two


def solution(mesh):
    return jax.shard_map(
        local,
        mesh=mesh,
        in_specs=(P(AXES, None),),
        out_specs=(P(AXES, None), P("band", None), P("band", None)),
        check_vma=False,
    )
```

```python
import functools
import math

import jax
import jax.numpy as jnp
import ml_dtypes
import numpy as np
from jax import lax
from jax.experimental import pallas as pl
from jax.experimental.pallas import tpu as pltpu
from jax.sharding import PartitionSpec as P

time_step = 0.2
viscosity = 0.4
forcing = 1.0
force_waves = 4.0

N = 8192
CUT = N // 3
DEV = 128
AXES = ("band", "sub")
f32 = jnp.float32
bf16 = jnp.bfloat16


def halves(table):
    table = np.asarray(table, np.float64).astype(np.float32)
    high = table.astype(ml_dtypes.bfloat16)
    low = (table - high.astype(np.float32)).astype(ml_dtypes.bfloat16)
    return np.stack([high, low])


def wave_of(t):
    return np.where(t % 2 == 1, -(t + 1) // 2, t // 2)


def slot_index():
    e, i = np.meshgrid(np.arange(16), np.arange(11), indexing="ij")
    return e + 16 * i


def backward_row_values(t, length):
    plen = length // 32
    p = np.arange(plen)
    ang = 2 * np.pi * ((wave_of(t)[..., None] * p) % plen) / plen
    gen = np.zeros(t.shape + (2, 2, plen))
    gen[..., 0, 0, :], gen[..., 1, 0, :] = np.cos(ang), -np.sin(ang)
    gen[..., 0, 1, :], gen[..., 1, 1, :] = np.sin(ang), np.cos(ang)
    ang = 2 * np.pi * ((16 * t[..., None] * p) % length) / length
    odd = (t % 2 == 1)[..., None]
    spe = np.zeros(t.shape + (2, 2, plen))
    spe[..., 0, 0, :], spe[..., 1, 0, :] = np.where(odd, 0, np.cos(ang)), np.where(odd, 0, -np.sin(ang))
    spe[..., 0, 1, :], spe[..., 1, 1, :] = np.where(odd, np.cos(ang), 0), np.where(odd, -np.sin(ang), 0)
    return np.stack([gen, spe]).reshape((2,) + t.shape + (2, 2 * plen))


def forward_row_tables():
    t = slot_index()
    p = np.arange(256)
    out = np.zeros((2, 16, 2, 12, 2, 256))
    ang = 2 * np.pi * ((wave_of(t)[:, :, None] * p) % 256) / 256
    out[0, :, 0, :11, 0], out[0, :, 0, :11, 1] = np.cos(ang), np.sin(ang)
    out[0, :, 1, :11, 0], out[0, :, 1, :11, 1] = -np.sin(ang), np.cos(ang)
    ang = 2 * np.pi * ((16 * t[:, :, None] * p) % N) / N
    odd = (t % 2 == 1)[:, :, None]
    out[1, :, 0, :11, 0], out[1, :, 1, :11, 0] = np.where(odd, 0, np.cos(ang)), np.where(odd, 0, -np.sin(ang))
    out[1, :, 0, :11, 1], out[1, :, 1, :11, 1] = np.where(odd, np.cos(ang), 0), np.where(odd, -np.sin(ang), 0)
    out = out.reshape(2, 16, 2, 3, 4, 512).transpose(0, 3, 1, 2, 4, 5).reshape(2, 384, 512)
    return halves(out[0]), halves(out[1])


def backward_field_tables():
    v = backward_row_values(slot_index(), N).transpose(0, 3, 2, 1, 4)
    return halves(v[:, :, :8].reshape(2, 256, 512)), halves(v[:, :, 8:].reshape(2, 96, 512))


def backward_next_tables():
    t = slot_index()
    v = backward_row_values(t, N)
    full = np.zeros((2, 3, 16, 8, 512))
    for ri in range(2):
        for i in range(11):
            full[:, i // 4, :, ri * 4 + i % 4 if i < 8 else ri * 3 + i - 8] = v[:, :, i, ri]
    v1 = backward_row_values(t, N // 2)
    one = np.zeros((2, 2, 16, 8, 256))
    v2 = backward_row_values(t, N // 4)
    two = np.zeros((2, 4, 16, 8, 128))
    for ri in range(2):
        for i in range(8):
            one[:, i % 2, :, (i // 2) * 2 + ri] = v1[:, :, i, ri]
        for i in range(4):
            two[:, i, :, 6 + ri] = v2[:, :, i, ri]
    full = full.reshape(2, 384, 512)
    return (
        halves(full[:, :256]),
        halves(full[:, 256:]),
        halves(one.reshape(2, 2, 128, 256)),
        halves(two.reshape(2, 4, 128, 128)),
    )


def row_twiddle(length):
    plen = length // 32
    ang = 2 * np.pi * np.arange(16)[:, None] * np.arange(plen) / length
    return (0.5 * np.stack([np.cos(ang), np.sin(ang)])).astype(np.float32)


def column_outer():
    ang = 2 * np.pi * ((np.arange(128)[:, None] * np.arange(128)) % 128) / 128
    c, s = np.cos(ang), np.sin(ang)
    return halves(np.block([[c, s], [-s, c]])), halves(np.block([[c, -s], [s, c]]))


def column_twiddle(rows_each, copies):
    length = DEV * rows_each
    ang = 2 * np.pi * np.arange(128)[:, None] * np.arange(rows_each) / length
    return np.stack([np.tile(np.cos(ang), (1, copies)), np.tile(np.sin(ang), (1, copies))]).astype(np.float32)


def column_inner(rows_each, copies, sign):
    j = np.arange(64)
    signed = np.where(j < 32, j, j - 64)
    ang = 2 * np.pi * ((signed[:, None] * np.arange(rows_each)) % rows_each) / rows_each
    keep = ((signed >= -rows_each // 2) & (signed < rows_each // 2))[:, None]
    c, s = np.cos(ang) * keep, np.sin(ang) * keep
    out = np.zeros((copies, 2, 2, 64, 2, copies, 2, rows_each))
    for m in range(copies):
        for k in range(2):
            out[m, 0, k, :, 0, m, k], out[m, 1, k, :, 0, m, k] = c, -s
            out[m, 0, k, :, 1, m, k], out[m, 1, k, :, 1, m, k] = s, c
    return out.reshape(copies * 256, 2 * copies * 2 * rows_each)


def cmul_const(a, ang):
    r, i = a
    n = round(ang / (math.pi / 16)) % 32
    if n == 0:
        return (r, i)
    if n == 8:
        return (-i, r)
    if n == 16:
        return (-r, -i)
    if n == 24:
        return (i, -r)
    h = math.sqrt(0.5)
    if n == 4:
        return ((r - i) * h, (r + i) * h)
    if n == 12:
        return ((r + i) * (-h), (r - i) * h)
    if n == 20:
        return ((i - r) * h, (r + i) * (-h))
    if n == 28:
        return ((r + i) * h, (i - r) * h)
    c, s = math.cos(n * math.pi / 16), math.sin(n * math.pi / 16)
    return (r * c - i * s, r * s + i * c)


def cadd(a, b):
    return (a[0] + b[0], a[1] + b[1])


def csub(a, b):
    return (a[0] - b[0], a[1] - b[1])


def fft_small(z, sign):
    n = len(z)
    if n == 1:
        return z
    if n == 2:
        return [cadd(z[0], z[1]), csub(z[0], z[1])]
    even, odd = fft_small(z[0::2], sign), fft_small(z[1::2], sign)
    out = [None] * n
    for k in range(n // 2):
        w = cmul_const(odd[k], sign * 2 * math.pi * k / n)
        out[k], out[k + n // 2] = cadd(even[k], w), csub(even[k], w)
    return out


def forward32(x):
    z = fft_small([(x[2 * m], x[2 * m + 1]) for m in range(16)], -1)
    ends = (z[0][0] + z[0][1], z[0][0] - z[0][1])
    rest = [None] * 16
    for k in range(1, 9):
        a, b = z[k], z[16 - k]
        even = (a[0] + b[0], a[1] - b[1])
        odd = (a[1] + b[1], b[0] - a[0])
        turned = cmul_const(odd, -2 * math.pi * k / 32)
        rest[k] = cadd(even, turned)
        if k < 8:
            other = csub(even, turned)
            rest[16 - k] = (other[0], -other[1])
    return ends, rest


def backward32(ends, rest):
    z = [None] * 16
    z[0] = (ends[0] + ends[1], ends[0] - ends[1])
    for k in range(1, 9):
        a, b = rest[k], rest[16 - k]
        even = (a[0] + b[0], a[1] - b[1])
        odd = cmul_const((a[0] - b[0], a[1] + b[1]), 2 * math.pi * k / 32)
        z[k] = (even[0] - odd[1], even[1] + odd[0])
        if k < 8:
            z[16 - k] = (even[0] + odd[1], odd[0] - even[1])
    z = fft_small(z, 1)
    out = []
    for m in range(16):
        out += [z[m][0], z[m][1]]
    return out


def split(x):
    high = x.astype(bf16)
    low = (x - high.astype(f32)).astype(bf16)
    return high, low


def mm(a, b, dims):
    return lax.dot_general(a, b, (dims, ((), ())), preferred_element_type=f32)


def dot_right(x, table, dims=((1,), (0,))):
    high, low = split(x)
    return mm(high, table[0], dims) + (mm(high, table[1], dims) + mm(low, table[0], dims))


def dot_left(table, x, dims=((1,), (0,))):
    high, low = split(x)
    return mm(table[0], high, dims) + (mm(table[0], low, dims) + mm(table[1], high, dims))


def pair(ref, *lead):
    return ref[(0,) + lead], ref[(1,) + lead]


MESH = pl.DeviceIdType.MESH
half_step = 0.5 * time_step
NN = ((1,), (0,))


def rows8(n):
    return pl.ds(pl.multiple_of(n * 8, 8), 8)


def kernel(names, *refs):
    count = len(names)
    ins, rest = refs[: count + 1], refs[count + 1 :]
    x_hbm, table_hbm = ins[0], ins[1:]
    section_ref, one_ref, two_ref = rest[:3]
    (x_v, y_ref, s1, r1, s2, r2, u4, up, s3, r3, s4, r4, vort_ref, next_ref, one_v, two_v, u1, u2) = rest[3:21]
    tables = rest[21 : 21 + count]
    send_sem, recv_sem, own_sem, load_sem, gather_send, gather_recv, out_sem = rest[21 + count :]
    T = dict(zip(names, tables))

    band, sub = lax.axis_index("band"), lax.axis_index("sub")
    me = band * 4 + sub
    y, z, c = band // 8, (band // 2) % 4, band % 2

    def peer(off):
        x2 = (sub + off % 4) % 4
        c2 = (c + (off // 4) % 2) % 2
        z2 = (z + (off // 8) % 4) % 4
        y2 = (y + off // 32) % 4
        return (y2 * 4 + z2) * 2 + c2, x2

    def load(n):
        if n < 0:
            return pltpu.make_async_copy(x_hbm, x_v, load_sem.at[count])
        return pltpu.make_async_copy(table_hbm[n], tables[n], load_sem.at[n])

    load(-1).start()
    for n in range(count):
        load(n).start()

    barrier = pltpu.get_barrier_semaphore()

    def greet(n, _):
        pl.semaphore_signal(barrier, inc=1, device_id=peer(n), device_id_type=MESH)
        return 0

    lax.fori_loop(1, DEV, greet, 0)

    def send(src, dst, m, sem):
        pltpu.make_async_copy(src.at[m, rows8(me)], dst.at[m, rows8(me)], own_sem.at[sem]).start()

        def one(n, _):
            to = peer((n * 37) % DEV)
            pltpu.make_async_remote_copy(
                src_ref=src.at[m, rows8(to[0] * 4 + to[1])],
                dst_ref=dst.at[m, rows8(me)],
                send_sem=send_sem.at[sem],
                recv_sem=recv_sem.at[sem],
                device_id=to,
                device_id_type=MESH,
            ).start()
            return 0

        lax.fori_loop(1, DEV, one, 0)

    def whole(src, dst, m, sem):
        return pltpu.make_async_remote_copy(
            src_ref=src.at[m, pl.ds(0, 8 * (DEV - 1))],
            dst_ref=dst.at[m, pl.ds(0, 8 * (DEV - 1))],
            send_sem=send_sem.at[sem],
            recv_sem=recv_sem.at[sem],
            device_id=peer(1),
            device_id_type=MESH,
        )

    def arrive(src, dst, m, sem):
        pltpu.make_async_copy(src.at[m, rows8(me)], dst.at[m, rows8(me)], own_sem.at[sem]).wait()
        whole(src, dst, m, sem).wait_recv()

    def put_forward(step, x, lanes, h, rows):
        ends, rest = forward32(x)
        y_ref[rows, pl.ds(128 * h, 128)] = ends[0]
        y_ref[rows, pl.ds(256 + 128 * h, 128)] = ends[1]
        tw = T["tw"]
        for k in range(1, 16):
            cs, sn = tw[0, k : k + 1, lanes], tw[1, k : k + 1, lanes]
            r, i = rest[k]
            to = rows8(k * 8 + step)
            y_ref[to, pl.ds(128 * h, 128)] = r * cs + i * sn
            y_ref[to, pl.ds(256 + 128 * h, 128)] = i * cs - r * sn

    def row_products(s):
        def product(step, _):
            v = y_ref[pl.ds(pl.multiple_of(step * 256, 256), 256), :]
            out = dot_left(pair(T["fg"]), v, ((1,), (1,)))
            for g in range(2):
                to = pl.ds(pl.multiple_of((2 * step + g) * 128, 128), 128)
                for m in range(3):
                    s[m, to, :] = out[128 * m : 128 * m + 128, 128 * g : 128 * g + 128]
            return 0

        lax.fori_loop(0, 4, product, 0)
        tail = dot_left(pair(T["fs"]), y_ref[:64, :], ((1,), (1,)))
        for m in range(3):
            s[m, :128, :64] = tail[128 * m : 128 * m + 128]

    load(-1).wait()
    for n in range(3):
        load(n).wait()

    def radix_first(step, _):
        rows = rows8(step)
        for h in range(2):
            x = [x_v[rows, pl.ds(256 * q + 128 * h, 128)] for q in range(32)]
            put_forward(step, x, pl.ds(128 * h, 128), h, rows)
        return 0

    lax.fori_loop(0, 8, radix_first, 0)
    row_products(s1)
    pl.semaphore_wait(barrier, DEV - 1)
    for m in range(3):
        send(s1, r1, m, m)
    for n in range(3, count):
        load(n).wait()

    ky = wave_y()
    factor = 2.0 * math.pi / N
    kappa_y = factor * ky.astype(f32)
    kept_y = (jnp.abs(ky) <= CUT).astype(f32)

    def forward_four(r, m):
        blocks = []
        for ii in range(4):
            both = [r[m, pl.ds(ri * 4 + ii, 128, stride=8), :] for ri in range(2)]
            blocks.append(jnp.concatenate(both, axis=0))
        out = dot_left(pair(T["fo"]), jnp.concatenate(blocks, axis=1))
        cs, sn = T["tc"][0], T["tc"][1]
        turned = []
        for ii in range(4):
            re, im = out[:128, 128 * ii : 128 * ii + 128], out[128:, 128 * ii : 128 * ii + 128]
            turned.append(jnp.concatenate([re * cs + im * sn, im * cs - re * sn], axis=1))
        out = dot_right(jnp.concatenate(turned, axis=0), pair(T["qf"]))
        return [(out[128 * ii : 128 * ii + 128, :128], out[128 * ii : 128 * ii + 128, 128:]) for ii in range(4)]

    def x_part(i):
        g, e = me // 16, me % 16
        t = e + 16 * i
        lane = lax.broadcasted_iota(jnp.int32, (1, 128), 1)
        k2 = 2 * g + lane // 64
        j2 = jnp.where(t % 2 == 1, -((t + 1) // 2), t // 2)
        kx = jnp.where(k2 == 0, 16 * t, k2 + 32 * j2)
        kappa_x = factor * kx.astype(f32)
        weight = jnp.where(kx == 0, 1.0, 2.0) / (float(N) * float(N))
        return kappa_x, (jnp.abs(kx) <= CUT).astype(f32), weight

    for m in range(3):
        arrive(s1, r1, m, m)
        four = forward_four(r1, m)
        for ii in range(4):
            vort_ref[4 * m + ii, :, :128], vort_ref[4 * m + ii, :, 128:] = four[ii]

        def slot(i, _):
            kappa_x, kept_x, weight = x_part(i)
            kept = kept_y * kept_x
            kappa_sq = kappa_x * kappa_x + kappa_y * kappa_y
            vr, vi = vort_ref[i, :, :128] * kept, vort_ref[i, :, 128:] * kept
            vort_ref[i, :, :128], vort_ref[i, :, 128:] = vr, vi
            positive = kappa_sq > 0
            inverse_sq = jnp.where(positive, 1.0 / jnp.where(positive, kappa_sq, 1.0), 0.0)
            sr, si = vr * inverse_sq, vi * inverse_sq
            kxw, kyw = kappa_x * weight, kappa_y * weight
            fields = [
                jnp.concatenate([-kyw * si, kyw * sr], axis=1),
                jnp.concatenate([kxw * si, -kxw * sr], axis=1),
                jnp.concatenate([-kxw * vi, kxw * vr], axis=1),
                jnp.concatenate([-kyw * vi, kyw * vr], axis=1),
            ]
            outs = column_backward(fields, T["tc"], T["bo"], pair(T["qb"]))
            for f in range(4):
                for ri in range(2):
                    s2[i, pl.ds(f * 2 + ri, 128, stride=8), :] = outs[f][128 * ri : 128 * ri + 128]
            send(s2, r2, i, 3 + i)
            return 0

        lax.fori_loop(4 * m, min(4 * m + 4, 11), slot, 0)

    def gather_rows(f, g, slots):
        parts = []
        for ri in range(2):
            for i in slots:
                parts.append(r2[i, pl.ds(g * 128 + f * 2 + ri, 16, stride=8), :])
        high, low = split(jnp.concatenate(parts, axis=0))
        return high.T, low.T

    def three(a, th, tl):
        return mm(a[0], th, NN) + (mm(a[0], tl, NN) + mm(a[1], th, NN))

    for part, (slots, table) in enumerate(((range(8), "g8"), (range(8, 11), "g3"))):
        for i in slots:
            arrive(s2, r2, i, 3 + i)
        gt = T[table]

        def pairs(n, _):
            f, step = n // 4, n % 4
            a, b = gather_rows(f, 2 * step, slots), gather_rows(f, 2 * step + 1, slots)
            both = [jnp.concatenate([a[j], b[j]], axis=0) for j in range(2)]
            out = three(both, gt[0, 0], gt[1, 0])
            to = pl.ds(pl.multiple_of(step * 256, 256), 256)
            u4[f, to, :] = out if part == 0 else u4[f, to, :] + out
            return 0

        lax.fori_loop(0, 16, pairs, 0)

        def edge(f, _):
            a = gather_rows(f, 0, slots)
            out = three((a[0][:64], a[1][:64]), gt[0, 1], gt[1, 1])
            up[f] = out if part == 0 else up[f] + out
            return 0

        lax.fori_loop(0, 4, edge, 0)

    def grid_values(u, edge, tw, step, lanes, ims, stride):
        ends = (edge[rows8(step), lanes], edge[rows8(step), ims])
        rest = [None] * 16
        for k in range(1, 16):
            cs, sn = tw[0, k : k + 1, lanes], tw[1, k : k + 1, lanes]
            at = rows8(k * stride + step)
            r, i = u[at, lanes], u[at, ims]
            rest[k] = (r * cs - i * sn, r * sn + i * cs)
        return backward32(ends, rest)

    def radix_product(step, _):
        row = lax.broadcasted_iota(jnp.int32, (8, 128), 0) + (me * 64 + step * 8)
        drive = forcing * jnp.sin((2.0 * math.pi * force_waves / N) * row.astype(f32))
        for h in range(2):
            lanes, ims = pl.ds(128 * h, 128), pl.ds(256 + 128 * h, 128)
            vals = [None] * 4
            for f in (0, 2, 1, 3):
                vals[f] = grid_values(u4.at[f], up.at[f], T["tw"], step, lanes, ims, 8)
                if f == 2:
                    total = [vals[0][q] * vals[2][q] for q in range(32)]
            x = [total[q] + vals[1][q] * vals[3][q] - drive for q in range(32)]
            put_forward(step, x, lanes, h, rows8(step))
        return 0

    lax.fori_loop(0, 8, radix_product, 0)
    row_products(s3)
    for m in range(3):
        send(s3, r3, m, 14 + m)

    inside_one = jnp.concatenate([(jnp.abs(ky) < 2048).astype(f32)] * 2, axis=1)
    inside_two = jnp.concatenate([(jnp.abs(ky) < 1024).astype(f32)] * 2, axis=1)
    for m in range(3):
        arrive(s3, r3, m, 14 + m)
        four = forward_four(r3, m)
        blocks = []
        for ii in range(4):
            i = 4 * m + ii
            if i == 11:
                continue
            kappa_x, kept_x, weight = x_part(i)
            kept = kept_y * kept_x
            kappa_sq = kappa_x * kappa_x + kappa_y * kappa_y
            vr, vi = vort_ref[i, :, :128], vort_ref[i, :, 128:]
            ar, ai = four[ii][0] * kept, four[ii][1] * kept
            nr = (vr + half_step * (-ar - viscosity * kappa_sq * vr)) * weight
            ni = (vi + half_step * (-ai - viscosity * kappa_sq * vi)) * weight
            blocks.append(jnp.concatenate([nr, ni], axis=1))
            if i < 8:
                next_ref[i] = blocks[-1]
        outs = column_backward(blocks, T["tc"], T["bo"], pair(T["qb"]))
        for ii, out in enumerate(outs):
            for ri in range(2):
                to, r = (m, ri * 4 + ii) if m < 2 else (3, ri * 3 + ii)
                s4[to, pl.ds(r, 128, stride=8), :] = out[128 * ri : 128 * ri + 128]
        if m < 2:
            send(s4, r4, m, 17 + m)
        if m == 1:
            for n in range(4):
                block = jnp.concatenate([next_ref[2 * n] * inside_one, next_ref[2 * n + 1] * inside_one], axis=1)
                (out,) = column_backward([block], T["tc1"], T["bo"], pair(T["q1"]))
                for ri in range(2):
                    s4[2, pl.ds(2 * n + ri, 128, stride=8), :] = out[128 * ri : 128 * ri + 128]
            send(s4, r4, 2, 19)
        if m == 2:
            block = jnp.concatenate([next_ref[n] * inside_two for n in range(4)], axis=1)
            (out,) = column_backward([block], T["tc2"], T["bo"], pair(T["q2"]))
            for ri in range(2):
                s4[3, pl.ds(6 + ri, 128, stride=8), :] = out[128 * ri : 128 * ri + 128]
            send(s4, r4, 3, 20)

    def transposed(m, g):
        high, low = split(r4[m, pl.ds(pl.multiple_of(g * 128, 128), 128), :])
        return high.T, low.T

    def coarse(m, table, u, each):
        copies = 64 // each

        def value(g, kind):
            a = transposed(m, g)
            total = None
            for n in range(copies):
                part = slice(n * 2 * each, (n + 1) * 2 * each)
                out = three((a[0][part], a[1][part]), table[0, kind, n], table[1, kind, n])
                total = out if total is None else total + out
            return total

        def product(g, _):
            u[pl.ds(pl.multiple_of(g * 2 * each, 2 * each), 2 * each), :] = value(g, 0)
            return 0

        lax.fori_loop(0, 8, product, 0)
        u[:each, :] = value(0, 1)[:each]

    def spread(value, out, each, base):
        rows = pl.ds(pl.multiple_of(sub * each, each), each)
        pltpu.make_async_copy(value, out.at[rows], out_sem.at[base // 3]).start()
        for n in range(3):
            pltpu.make_async_remote_copy(
                src_ref=value,
                dst_ref=out.at[rows],
                send_sem=gather_send.at[base + n],
                recv_sem=gather_recv.at[base + n],
                device_id=(band, (sub + n + 1) % 4),
                device_id_type=MESH,
            ).start()

    def gathered(value, out, each, base):
        rows = pl.ds(pl.multiple_of(sub * each, each), each)
        pltpu.make_async_copy(value, out.at[rows], out_sem.at[base // 3]).wait()
        for n in range(3):
            copy = pltpu.make_async_remote_copy(
                src_ref=value,
                dst_ref=out.at[rows],
                send_sem=gather_send.at[base + n],
                recv_sem=gather_recv.at[base + n],
                device_id=(band, (sub + n + 1) % 4),
                device_id_type=MESH,
            )
            copy.wait_send()
            copy.wait_recv()

    arrive(s4, r4, 0, 17)
    arrive(s4, r4, 1, 18)
    u0, u0p = u4.at[0], up.at[0]

    def section_first(step, _):
        parts = [[transposed(m, 2 * step + g) for m in range(2)] for g in range(2)]
        both = [
            jnp.concatenate([jnp.concatenate([parts[g][0][j], parts[g][1][j]], axis=1) for g in range(2)], axis=0)
            for j in range(2)
        ]
        u0[pl.ds(pl.multiple_of(step * 256, 256), 256), :] = three(both, T["e8"][0, 0], T["e8"][1, 0])
        return 0

    lax.fori_loop(0, 4, section_first, 0)
    parts = [transposed(m, 0) for m in range(2)]
    both = [jnp.concatenate([parts[0][j][:64], parts[1][j][:64]], axis=1) for j in range(2)]
    u0p[...] = three(both, T["e8"][0, 1], T["e8"][1, 1])

    arrive(s4, r4, 2, 19)
    coarse(2, T["c1"], u1, 32)

    def radix_one(step, _):
        out = grid_values(u1, u1, T["tw1"], step, pl.ds(0, 128), pl.ds(128, 128), 4)
        for q in range(32):
            one_v[rows8(step), pl.ds(128 * q, 128)] = out[q]
        return 0

    lax.fori_loop(0, 4, radix_one, 0)
    spread(one_v, one_ref, 32, 0)

    arrive(s4, r4, 3, 20)
    coarse(3, T["c2"], u2, 16)

    def radix_two(step, _):
        out = grid_values(u2, u2, T["tw2"], step, pl.ds(0, 64), pl.ds(64, 64), 2)
        for q in range(16):
            two_v[rows8(step), pl.ds(128 * q, 128)] = jnp.concatenate([out[2 * q], out[2 * q + 1]], axis=1)
        return 0

    lax.fori_loop(0, 2, radix_two, 0)
    spread(two_v, two_ref, 16, 3)

    def section_last(step, _):
        a = [transposed(3, 2 * step + g) for g in range(2)]
        both = [jnp.concatenate([a[0][j], a[1][j]], axis=0) for j in range(2)]
        to = pl.ds(pl.multiple_of(step * 256, 256), 256)
        u0[to, :] = u0[to, :] + three(both, T["e3"][0, 0], T["e3"][1, 0])
        return 0

    lax.fori_loop(0, 4, section_last, 0)
    a = transposed(3, 0)
    u0p[...] = u0p[...] + three((a[0][:64], a[1][:64]), T["e3"][0, 1], T["e3"][1, 1])

    def radix_section(step, _):
        for h in range(2):
            lanes, ims = pl.ds(128 * h, 128), pl.ds(256 + 128 * h, 128)
            out = grid_values(u0, u0p, T["tw"], step, lanes, ims, 8)
            for q in range(32):
                x_v[rows8(step), pl.ds(256 * q + 128 * h, 128)] = out[q]
        return 0

    lax.fori_loop(0, 8, radix_section, 0)
    final = pltpu.make_async_copy(x_v, section_ref, out_sem.at[2])
    final.start()
    for m in range(3):
        whole(s1, r1, m, m).wait_send()
        whole(s3, r3, m, 14 + m).wait_send()
    for i in range(11):
        whole(s2, r2, i, 3 + i).wait_send()
    for m in range(4):
        whole(s4, r4, m, 17 + m).wait_send()
    gathered(one_v, one_ref, 32, 0)
    gathered(two_v, two_ref, 16, 3)
    final.wait()


def wave_y():
    k = lax.broadcasted_iota(jnp.int32, (128, 128), 0)
    lane = lax.broadcasted_iota(jnp.int32, (128, 128), 1)
    j = lane % 64
    return k + 128 * jnp.where(j < 32, j, j - 64)


def column_backward(fields, tc_ref, bo_ref, qb_table):
    stacked = jnp.concatenate(fields, axis=0) if len(fields) > 1 else fields[0]
    u = dot_right(stacked, qb_table)
    c, s = tc_ref[0], tc_ref[1]
    cols = []
    for n in range(len(fields)):
        r, im = u[128 * n : 128 * n + 128, :128], u[128 * n : 128 * n + 128, 128:]
        cols.append(jnp.concatenate([r * c - im * s, r * s + im * c], axis=0))
    joined = jnp.concatenate(cols, axis=1) if len(cols) > 1 else cols[0]
    out = dot_left(pair(bo_ref), joined)
    return [out[:, 128 * n : 128 * n + 128] for n in range(len(fields))]


def all_tables():
    fg, fs = forward_row_tables()
    g8, g3 = backward_field_tables()
    e8, e3, c1, c2 = backward_next_tables()
    fo, bo = column_outer()
    inner = column_inner(64, 1, 1)
    return {
        "tw": row_twiddle(N),
        "fg": fg,
        "fs": fs,
        "fo": fo,
        "tc": column_twiddle(64, 2),
        "qf": halves(inner.T),
        "bo": bo,
        "qb": halves(inner),
        "g8": g8,
        "g3": g3,
        "tc1": column_twiddle(32, 4),
        "tc2": column_twiddle(16, 8),
        "q1": halves(column_inner(32, 2, 1)),
        "q2": halves(column_inner(16, 4, 1)),
        "e8": e8,
        "e3": e3,
        "c1": c1,
        "c2": c2,
        "tw1": row_twiddle(N // 2),
        "tw2": row_twiddle(N // 4),
    }


def local(vorticity):
    tables = all_tables()
    names = tuple(tables)
    anywhere = pl.BlockSpec(memory_space=pl.ANY)
    shapes = [(64, N), (128, N // 2), (64, N // 4)]
    part = lambda n: (n, 8 * DEV, 128)
    scratch = [(64, N), (1024, 512), part(3), part(3), part(11), part(11), (4, 1024, 512), (4, 64, 512)]
    scratch += [part(3), part(3), part(4), part(4), (12, 128, 256), (8, 128, 256)]
    scratch += [(32, N // 2), (16, N // 4), (512, 256), (256, 128)]
    dma = pltpu.SemaphoreType.DMA
    section, one, two = pl.pallas_call(
        functools.partial(kernel, names),
        out_shape=[jax.ShapeDtypeStruct(s, f32) for s in shapes],
        in_specs=[anywhere] * (1 + len(names)),
        out_specs=[anywhere] * 3,
        scratch_shapes=[pltpu.VMEM(s, f32) for s in scratch]
        + [pltpu.VMEM(t.shape, t.dtype) for t in tables.values()]
        + [dma((21,)), dma((21,)), dma((21,)), dma((len(names) + 1,)), dma((6,)), dma((6,)), dma((3,))],
        compiler_params=pltpu.CompilerParams(
            collective_id=0, has_side_effects=True, vmem_limit_bytes=60 * 2**20
        ),
    )(vorticity, *[jnp.asarray(t) for t in tables.values()])
    return section, one, two


def solution(mesh):
    return jax.shard_map(
        local,
        mesh=mesh,
        in_specs=(P(AXES, None),),
        out_specs=(P(AXES, None), P("band", None), P("band", None)),
        check_vma=False,
    )
```

```python
import functools
import math

import jax
import jax.numpy as jnp
import ml_dtypes
import numpy as np
from jax import lax
from jax.experimental import pallas as pl
from jax.experimental.pallas import tpu as pltpu
from jax.sharding import PartitionSpec as P

time_step = 0.2
viscosity = 0.4
forcing = 1.0
force_waves = 4.0

N = 8192
CUT = N // 3
DEV = 128
AXES = ("band", "sub")
f32 = jnp.float32
bf16 = jnp.bfloat16


def halves(table):
    table = np.asarray(table, np.float64).astype(np.float32)
    high = table.astype(ml_dtypes.bfloat16)
    low = (table - high.astype(np.float32)).astype(ml_dtypes.bfloat16)
    return np.stack([high, low])


def wave_of(t):
    return np.where(t % 2 == 1, -(t + 1) // 2, t // 2)


def slot_index():
    e, i = np.meshgrid(np.arange(16), np.arange(11), indexing="ij")
    return e + 16 * i


def backward_row_values(t, length):
    plen = length // 32
    p = np.arange(plen)
    ang = 2 * np.pi * ((wave_of(t)[..., None] * p) % plen) / plen
    gen = np.zeros(t.shape + (2, 2, plen))
    gen[..., 0, 0, :], gen[..., 1, 0, :] = np.cos(ang), -np.sin(ang)
    gen[..., 0, 1, :], gen[..., 1, 1, :] = np.sin(ang), np.cos(ang)
    ang = 2 * np.pi * ((16 * t[..., None] * p) % length) / length
    odd = (t % 2 == 1)[..., None]
    spe = np.zeros(t.shape + (2, 2, plen))
    spe[..., 0, 0, :], spe[..., 1, 0, :] = np.where(odd, 0, np.cos(ang)), np.where(odd, 0, -np.sin(ang))
    spe[..., 0, 1, :], spe[..., 1, 1, :] = np.where(odd, np.cos(ang), 0), np.where(odd, -np.sin(ang), 0)
    return np.stack([gen, spe]).reshape((2,) + t.shape + (2, 2 * plen))


def thirds(table):
    left = np.asarray(table, np.float64).astype(np.float32)
    out = []
    for _ in range(3):
        out.append(left.astype(ml_dtypes.bfloat16))
        left = left - out[-1].astype(np.float32)
    return np.stack(out)


def stack3(pair_of):
    return np.concatenate([pair_of[0], pair_of[1], pair_of[0]], axis=1)


def forward_row_tables():
    t = slot_index()
    p = np.arange(256)
    out = np.zeros((2, 16, 2, 12, 2, 256))
    ang = 2 * np.pi * ((wave_of(t)[:, :, None] * p) % 256) / 256
    out[0, :, 0, :11, 0], out[0, :, 0, :11, 1] = np.cos(ang), np.sin(ang)
    out[0, :, 1, :11, 0], out[0, :, 1, :11, 1] = -np.sin(ang), np.cos(ang)
    ang = 2 * np.pi * ((16 * t[:, :, None] * p) % N) / N
    odd = (t % 2 == 1)[:, :, None]
    out[1, :, 0, :11, 0], out[1, :, 1, :11, 0] = np.where(odd, 0, np.cos(ang)), np.where(odd, 0, -np.sin(ang))
    out[1, :, 0, :11, 1], out[1, :, 1, :11, 1] = np.where(odd, np.cos(ang), 0), np.where(odd, -np.sin(ang), 0)
    full = np.zeros((2, 3, 16, 8, 512))
    for ri in range(2):
        for i in range(11):
            full[:, i // 4, :, ri * 4 + i % 4 if i < 8 else ri * 3 + i - 8] = out[:, :, ri, i].reshape(2, 16, 512)
    full = np.moveaxis(thirds(full.reshape(2, 384, 512)), 0, 1).reshape(2, 1152, 512)
    return full[0], full[1]


def backward_field_tables():
    v = backward_row_values(slot_index(), N).transpose(0, 3, 2, 1, 4)
    return halves(v[:, :, :8].reshape(2, 256, 512)), stack3(halves(v[:, :, 8:].reshape(2, 96, 512)))


def backward_next_tables():
    t = slot_index()
    v = backward_row_values(t, N)
    full = np.zeros((2, 3, 16, 8, 512))
    for ri in range(2):
        for i in range(11):
            full[:, i // 4, :, ri * 4 + i % 4 if i < 8 else ri * 3 + i - 8] = v[:, :, i, ri]
    v1 = backward_row_values(t, N // 2)
    one = np.zeros((2, 2, 16, 8, 256))
    v2 = backward_row_values(t, N // 4)
    two = np.zeros((2, 4, 16, 8, 128))
    for ri in range(2):
        for i in range(8):
            one[:, i % 2, :, (i // 2) * 2 + ri] = v1[:, :, i, ri]
        for i in range(4):
            two[:, i, :, ri] = v2[:, :, i, ri]
    full = full.reshape(2, 384, 512)
    return (
        halves(full[:, :256]),
        halves(full[:, 256:]),
        halves(one.reshape(2, 256, 256)),
        halves(two.reshape(2, 512, 128)),
    )


def row_twiddle(length):
    plen = length // 32
    ang = 2 * np.pi * np.arange(16)[:, None] * np.arange(plen) / length
    return (0.5 * np.stack([np.cos(ang), np.sin(ang)])).astype(np.float32)


def column_outer():
    ang = 2 * np.pi * ((np.arange(128)[:, None] * np.arange(128)) % 128) / 128
    c, s = np.cos(ang), np.sin(ang)
    return np.block([[c, s], [-s, c]]), np.block([[c, -s], [s, c]])


def column_twiddle(rows_each, copies):
    length = DEV * rows_each
    ang = 2 * np.pi * np.arange(128)[:, None] * np.arange(rows_each) / length
    return np.stack([np.tile(np.cos(ang), (1, copies)), np.tile(np.sin(ang), (1, copies))]).astype(np.float32)


def column_inner(rows_each, copies, sign):
    j = np.arange(64)
    signed = np.where(j < 32, j, j - 64)
    ang = 2 * np.pi * ((signed[:, None] * np.arange(rows_each)) % rows_each) / rows_each
    keep = ((signed >= -rows_each // 2) & (signed < rows_each // 2))[:, None]
    c, s = np.cos(ang) * keep, np.sin(ang) * keep
    out = np.zeros((copies, 2, 2, 64, 2, copies, 2, rows_each))
    for m in range(copies):
        for k in range(2):
            out[m, 0, k, :, 0, m, k], out[m, 1, k, :, 0, m, k] = c, -s
            out[m, 0, k, :, 1, m, k], out[m, 1, k, :, 1, m, k] = s, c
    return out.reshape(copies * 256, 2 * copies * 2 * rows_each)


def cmul_const(a, ang):
    r, i = a
    n = round(ang / (math.pi / 16)) % 32
    if n == 0:
        return (r, i)
    if n == 8:
        return (-i, r)
    if n == 16:
        return (-r, -i)
    if n == 24:
        return (i, -r)
    h = math.sqrt(0.5)
    if n == 4:
        return ((r - i) * h, (r + i) * h)
    if n == 12:
        return ((r + i) * (-h), (r - i) * h)
    if n == 20:
        return ((i - r) * h, (r + i) * (-h))
    if n == 28:
        return ((r + i) * h, (i - r) * h)
    c, s = math.cos(n * math.pi / 16), math.sin(n * math.pi / 16)
    return (r * c - i * s, r * s + i * c)


def cadd(a, b):
    return (a[0] + b[0], a[1] + b[1])


def csub(a, b):
    return (a[0] - b[0], a[1] - b[1])


def fft_small(z, sign):
    n = len(z)
    if n == 1:
        return z
    if n == 2:
        return [cadd(z[0], z[1]), csub(z[0], z[1])]
    even, odd = fft_small(z[0::2], sign), fft_small(z[1::2], sign)
    out = [None] * n
    for k in range(n // 2):
        w = cmul_const(odd[k], sign * 2 * math.pi * k / n)
        out[k], out[k + n // 2] = cadd(even[k], w), csub(even[k], w)
    return out


def forward32(x):
    z = fft_small([(x[2 * m], x[2 * m + 1]) for m in range(16)], -1)
    ends = (z[0][0] + z[0][1], z[0][0] - z[0][1])
    rest = [None] * 16
    for k in range(1, 9):
        a, b = z[k], z[16 - k]
        even = (a[0] + b[0], a[1] - b[1])
        odd = (a[1] + b[1], b[0] - a[0])
        turned = cmul_const(odd, -2 * math.pi * k / 32)
        rest[k] = cadd(even, turned)
        if k < 8:
            other = csub(even, turned)
            rest[16 - k] = (other[0], -other[1])
    return ends, rest


def backward32(ends, rest):
    z = [None] * 16
    z[0] = (ends[0] + ends[1], ends[0] - ends[1])
    for k in range(1, 9):
        a, b = rest[k], rest[16 - k]
        even = (a[0] + b[0], a[1] - b[1])
        odd = cmul_const((a[0] - b[0], a[1] + b[1]), 2 * math.pi * k / 32)
        z[k] = (even[0] - odd[1], even[1] + odd[0])
        if k < 8:
            z[16 - k] = (even[0] + odd[1], odd[0] - even[1])
    z = fft_small(z, 1)
    out = []
    for m in range(16):
        out += [z[m][0], z[m][1]]
    return out


def split(x):
    high = x.astype(bf16)
    low = (x - high.astype(f32)).astype(bf16)
    return high, low


def mm(a, b, dims):
    return lax.dot_general(a, b, (dims, ((), ())), preferred_element_type=f32)


def dot_right(x, table, dims=((1,), (0,))):
    high, low = split(x)
    return mm(high, table[0], dims) + (mm(high, table[1], dims) + mm(low, table[0], dims))


def dot_left(table, x, dims=((1,), (0,))):
    high, low = split(x)
    return mm(table[0], high, dims) + (mm(table[0], low, dims) + mm(table[1], high, dims))


def pair(ref, *lead):
    return ref[(0,) + lead], ref[(1,) + lead]


MESH = pl.DeviceIdType.MESH
half_step = 0.5 * time_step
NN = ((1,), (0,))


def rows8(n):
    return pl.ds(pl.multiple_of(n * 8, 8), 8)


def kernel(names, *refs):
    count = len(names)
    ins, rest = refs[: count + 1], refs[count + 1 :]
    x_hbm, table_hbm = ins[0], ins[1:]
    section_ref, one_ref, two_ref = rest[:3]
    (x_v, y_ref, s1, r1, s2, r2, u4, up, s3, r3, s4, r4, vort_ref, next_ref, one_v, two_v, u1, u2) = rest[3:21]
    tables = rest[21 : 21 + count]
    send_sem, recv_sem, own_sem, load_sem, gather_send, gather_recv, out_sem = rest[21 + count :]
    T = dict(zip(names, tables))

    band, sub = lax.axis_index("band"), lax.axis_index("sub")
    me = band * 4 + sub
    y, z, c = band // 8, (band // 2) % 4, band % 2

    def wrap(v):
        return jnp.where(v >= 4, v - 4, v)

    xs, cs = [sub] + [wrap(sub + k) for k in range(1, 4)], [c, 1 - c]

    def each_peer(act, first=0, last=16):
        def group(dy, dz, skip):
            for k in range(4):
                base = (wrap(wrap(y + dy) + k) * 4 + wrap(wrap(z + dz) + k)) * 2
                for d in range(2):
                    if not (skip and k == 0 and d == 0):
                        act(base + cs[d], xs[k])

        if first == 0:
            group(0, 0, True)

        def body(w, _):
            dy = w // 4
            group(dy, w - 4 * dy, False)
            return 0

        lax.fori_loop(max(first, 1), last, body, 0)

    def load(n):
        if n < 0:
            return pltpu.make_async_copy(x_hbm, x_v, load_sem.at[count])
        return pltpu.make_async_copy(table_hbm[n], tables[n], load_sem.at[n])

    load(-1).start()
    for n in range(count):
        load(n).start()

    barrier = pltpu.get_barrier_semaphore()

    def greet(*to):
        pl.semaphore_signal(barrier, inc=1, device_id=to, device_id_type=MESH)

    each_peer(greet)

    def rows_of(n, count):
        return pl.ds(pl.multiple_of(n * 8, 8), count)

    def send(src, dst, m, sem, each=8):
        own = rows_of(me, each)
        pltpu.make_async_copy(src.at[m, own], dst.at[m, own], own_sem.at[sem]).start()

        def one(*to):
            pltpu.make_async_remote_copy(
                src_ref=src.at[m, rows_of(to[0] * 4 + to[1], each)],
                dst_ref=dst.at[m, own],
                send_sem=send_sem.at[sem],
                recv_sem=recv_sem.at[sem],
                device_id=to,
                device_id_type=MESH,
            ).start()

        each_peer(one)

    def whole(src, dst, m, sem, each=8):
        return pltpu.make_async_remote_copy(
            src_ref=src.at[m, pl.ds(0, each * (DEV - 1))],
            dst_ref=dst.at[m, pl.ds(0, each * (DEV - 1))],
            send_sem=send_sem.at[sem],
            recv_sem=recv_sem.at[sem],
            device_id=(band, xs[1]),
            device_id_type=MESH,
        )

    def arrive(src, dst, m, sem, each=8):
        own = rows_of(me, each)
        pltpu.make_async_copy(src.at[m, own], dst.at[m, own], own_sem.at[sem]).wait()
        whole(src, dst, m, sem, each).wait_recv()

    def put_forward(step, x, lanes, h, rows):
        ends, rest = forward32(x)
        y_ref[rows, pl.ds(128 * h, 128)] = ends[0]
        y_ref[rows, pl.ds(256 + 128 * h, 128)] = ends[1]
        tw = T["tw"]
        for k in range(1, 16):
            cs, sn = tw[0, k : k + 1, lanes], tw[1, k : k + 1, lanes]
            r, i = rest[k]
            to = rows8(k * 8 + step)
            y_ref[to, pl.ds(128 * h, 128)] = r * cs + i * sn
            y_ref[to, pl.ds(256 + 128 * h, 128)] = i * cs - r * sn

    def row_products(s, r, base, pieces, ready):
        def value(table, v):
            total = None
            for n, part in enumerate(split_n(v, pieces)):
                out = mm(table[: 384 * (pieces - n)], part, ((1,), (1,)))
                for k in range(pieces - n):
                    one = out[384 * k : 384 * k + 384]
                    total = one if total is None else total + one
            return total

        def product(step, _):
            out = value(T["fg"], y_ref[pl.ds(pl.multiple_of(step * 256, 256), 256), :])
            for g in range(2):
                to = pl.ds(pl.multiple_of((2 * step + g) * 128, 128), 128)
                for m in range(3):
                    s[m, to, :] = out[128 * m : 128 * m + 128, 128 * g : 128 * g + 128]
            return 0

        lax.fori_loop(0, 4, product, 0)
        tail = value(T["fs"], y_ref[:64, :])
        for m in range(3):
            s[m, :128, :64] = tail[128 * m : 128 * m + 128]
        ready()
        for m in range(3):
            send(s, r, m, base + m, 8 if m < 2 else 6)

    load(-1).wait()
    for n in range(3):
        load(n).wait()

    def radix_first(step, _):
        rows = rows8(step)
        for h in range(2):
            x = [x_v[rows, pl.ds(256 * q + 128 * h, 128)] for q in range(32)]
            put_forward(step, x, pl.ds(128 * h, 128), h, rows)
        return 0

    lax.fori_loop(0, 8, radix_first, 0)
    row_products(s1, r1, 0, 3, lambda: pl.semaphore_wait(barrier, DEV - 1))
    for n in range(3, count):
        load(n).wait()

    ky = wave_y()
    factor = 2.0 * math.pi / N
    kappa_y = factor * ky.astype(f32)
    kept_y = (jnp.abs(ky) <= CUT).astype(f32)

    def forward_four(r, m, pieces):
        blocks, four = [], 4 if m < 2 else 3
        for ii in range(four):
            both = [r[m, pl.ds(ri * four + ii, 128, stride=8), :] for ri in range(2)]
            blocks.append(jnp.concatenate(both, axis=0))
        parts = split_n(jnp.concatenate(blocks, axis=1), pieces)
        out = sum(mm(T["fo"][k], parts[n], NN) for n in range(pieces) for k in range(pieces - n))
        cs, sn = T["tc"][0], T["tc"][1]
        turned = []
        for ii in range(four):
            re, im = out[:128, 128 * ii : 128 * ii + 128], out[128:, 128 * ii : 128 * ii + 128]
            turned.append(jnp.concatenate([re * cs + im * sn, im * cs - re * sn], axis=1))
        parts = split_n(jnp.concatenate(turned, axis=0), pieces)
        out = sum(mm(parts[n], T["qf"][k], NN) for n in range(pieces) for k in range(pieces - n))
        return [(out[128 * ii : 128 * ii + 128, :128], out[128 * ii : 128 * ii + 128, 128:]) for ii in range(four)]

    def x_part(i):
        g, e = me // 16, me % 16
        t = e + 16 * i
        lane = lax.broadcasted_iota(jnp.int32, (1, 128), 1)
        k2 = 2 * g + lane // 64
        j2 = jnp.where(t % 2 == 1, -((t + 1) // 2), t // 2)
        kx = jnp.where(k2 == 0, 16 * t, k2 + 32 * j2)
        kappa_x = factor * kx.astype(f32)
        weight = jnp.where(kx == 0, 1.0, 2.0) / (float(N) * float(N))
        return kappa_x, (jnp.abs(kx) <= CUT).astype(f32), weight

    for m in range(3):
        arrive(s1, r1, m, m, 8 if m < 2 else 6)
        four = forward_four(r1, m, 3)
        for ii in range(len(four)):
            vort_ref[4 * m + ii, :, :128], vort_ref[4 * m + ii, :, 128:] = four[ii]

        def slot(i, _):
            kappa_x, kept_x, weight = x_part(i)
            kept = kept_y * kept_x
            kappa_sq = kappa_x * kappa_x + kappa_y * kappa_y
            vr, vi = vort_ref[i, :, :128] * kept, vort_ref[i, :, 128:] * kept
            vort_ref[i, :, :128], vort_ref[i, :, 128:] = vr, vi
            positive = kappa_sq > 0
            inverse_sq = jnp.where(positive, 1.0 / jnp.where(positive, kappa_sq, 1.0), 0.0)
            sr, si = vr * inverse_sq, vi * inverse_sq
            kxw, kyw = kappa_x * weight, kappa_y * weight
            fields = [
                jnp.concatenate([-kyw * si, kyw * sr], axis=1),
                jnp.concatenate([kxw * si, -kxw * sr], axis=1),
                jnp.concatenate([-kxw * vi, kxw * vr], axis=1),
                jnp.concatenate([-kyw * vi, kyw * vr], axis=1),
            ]
            outs = column_backward(fields, T["tc"], T["bo"], pair(T["qb"]))
            for f in range(4):
                for ri in range(2):
                    s2[i, pl.ds(f * 2 + ri, 128, stride=8), :] = outs[f][128 * ri : 128 * ri + 128]
            send(s2, r2, i, 3 + i)
            return 0

        lax.fori_loop(4 * m, min(4 * m + 4, 11), slot, 0)

    def gather_rows(f, g, slots):
        parts = []
        for ri in range(2):
            for i in slots:
                parts.append(r2[i, pl.ds(g * 128 + f * 2 + ri, 16, stride=8), :])
        return split(jnp.concatenate(parts, axis=0))

    def three(a, th, tl):
        return mm(a[0], th, NN) + (mm(a[0], tl, NN) + mm(a[1], th, NN))

    for part, (slots, table) in enumerate(((range(8), "g8"), (range(8, 11), "g3"))):
        for i in slots:
            arrive(s2, r2, i, 3 + i)
        gt = T[table]

        def value(f, gs, kind, rows):
            got = [gather_rows(f, g, slots) for g in gs]
            if part == 0:
                both = [jnp.concatenate([a[j].T[:rows] for a in got], axis=0) for j in range(2)]
                return three(both, gt[0, kind], gt[1, kind])
            both = [jnp.concatenate([a[0], a[0], a[1]], axis=0).T[:rows] for a in got]
            return mm(jnp.concatenate(both, axis=0), gt[kind], NN)

        def pairs(n, _):
            f, step = n // 4, n % 4
            out = value(f, (2 * step, 2 * step + 1), 0, 128)
            to = pl.ds(pl.multiple_of(step * 256, 256), 256)
            u4[f, to, :] = out if part == 0 else u4[f, to, :] + out
            return 0

        lax.fori_loop(0, 16, pairs, 0)

        def edge(f, _):
            out = value(f, (0,), 1, 64)
            up[f] = out if part == 0 else up[f] + out
            return 0

        lax.fori_loop(0, 4, edge, 0)

    def grid_values(u, edge, tw, step, lanes, ims, stride):
        ends = (edge[rows8(step), lanes], edge[rows8(step), ims])
        rest = [None] * 16
        for k in range(1, 16):
            cs, sn = tw[0, k : k + 1, lanes], tw[1, k : k + 1, lanes]
            at = rows8(k * stride + step)
            r, i = u[at, lanes], u[at, ims]
            rest[k] = (r * cs - i * sn, r * sn + i * cs)
        return backward32(ends, rest)

    def radix_product(step, _):
        row = lax.broadcasted_iota(jnp.int32, (8, 128), 0) + (me * 64 + step * 8)
        drive = forcing * jnp.sin((2.0 * math.pi * force_waves / N) * row.astype(f32))
        for h in range(2):
            lanes, ims = pl.ds(128 * h, 128), pl.ds(256 + 128 * h, 128)
            vals = [None] * 4
            for f in (0, 2, 1, 3):
                vals[f] = grid_values(u4.at[f], up.at[f], T["tw"], step, lanes, ims, 8)
                if f == 2:
                    total = [vals[0][q] * vals[2][q] for q in range(32)]
            x = [total[q] + vals[1][q] * vals[3][q] - drive for q in range(32)]
            put_forward(step, x, lanes, h, rows8(step))
        return 0

    lax.fori_loop(0, 8, radix_product, 0)
    row_products(s3, r3, 14, 2, lambda: None)

    inside_one = jnp.concatenate([(jnp.abs(ky) < 2048).astype(f32)] * 2, axis=1)
    inside_two = jnp.concatenate([(jnp.abs(ky) < 1024).astype(f32)] * 2, axis=1)

    def whole_blocks(m, blocks):
        outs = column_backward(blocks, T["tc"], T["bo"], pair(T["qb"]))
        for ii, out in enumerate(outs):
            for ri in range(2):
                to, r = (m, ri * 4 + ii) if m < 2 else (3, ri * 3 + ii)
                s4[to, pl.ds(r, 128, stride=8), :] = out[128 * ri : 128 * ri + 128]

    for m in range(3):
        arrive(s3, r3, m, 14 + m, 8 if m < 2 else 6)
        blocks = []
        for ii, (ar, ai) in enumerate(forward_four(r3, m, 2)):
            i = 4 * m + ii
            kappa_x, kept_x, weight = x_part(i)
            kept = kept_y * kept_x
            kappa_sq = kappa_x * kappa_x + kappa_y * kappa_y
            vr, vi = vort_ref[i, :, :128], vort_ref[i, :, 128:]
            ar, ai = ar * kept, ai * kept
            nr = (vr + half_step * (-ar - viscosity * kappa_sq * vr)) * weight
            ni = (vi + half_step * (-ai - viscosity * kappa_sq * vi)) * weight
            blocks.append(jnp.concatenate([nr, ni], axis=1))
            if i < 8:
                next_ref[i] = blocks[-1]
        if m == 0:
            whole_blocks(0, blocks)
            send(s4, r4, 0, 17)
        if m == 1:
            for n in range(4):
                block = jnp.concatenate([next_ref[2 * n] * inside_one, next_ref[2 * n + 1] * inside_one], axis=1)
                (out,) = column_backward([block], T["tc1"], T["bo"], pair(T["q1"]))
                for ri in range(2):
                    s4[2, pl.ds(2 * n + ri, 128, stride=8), :] = out[128 * ri : 128 * ri + 128]
            send(s4, r4, 2, 19)
            block = jnp.concatenate([next_ref[n] * inside_two for n in range(4)], axis=1)
            (out,) = column_backward([block], T["tc2"], T["bo"], pair(T["q2"]))
            for ri in range(2):
                s4[4, pl.ds(ri, 128, stride=8), :] = out[128 * ri : 128 * ri + 128]
            send(s4, r4, 4, 21, 2)
            whole_blocks(1, blocks)
            send(s4, r4, 1, 18)
        if m == 2:
            whole_blocks(2, blocks)
            send(s4, r4, 3, 20, 6)

    def transposed(m, g, valid=8):
        block = r4[m, pl.ds(pl.multiple_of(g * 128, 128), 128), :]
        if valid < 8:
            row = lax.broadcasted_iota(jnp.int32, (128, 128), 0) % 8
            block = jnp.where(row < valid, block, 0.0)
        high, low = split(block)
        return high.T, low.T

    def coarse(m, table, u, each, valid):
        copies = 64 // each

        def value(gs, kind):
            both = [[], []]
            for g in gs:
                a = transposed(m, g, valid)
                for j in range(2):
                    parts = [a[j][n * 2 * each : (n + 1) * 2 * each] for n in range(copies)]
                    both[j].append(jnp.concatenate(parts, axis=1))
            both = [jnp.concatenate(v, axis=0) for v in both]
            return three(both, table[0, kind], table[1, kind])

        def product(n, _):
            out = value([4 * n + k for k in range(4)], 0)
            u[pl.ds(pl.multiple_of(n * 8 * each, 8 * each), 8 * each), :] = out
            return 0

        lax.fori_loop(0, 2, product, 0)
        u[:each, :] = value([0], 1)[:each]

    right, left = (sub + 1) % 4, (sub + 3) % 4

    def ring(value, out, each, base):
        def rows(owner, start, size):
            return out.at[pl.ds(pl.multiple_of(owner * each + start, 8), size)]

        def remote(src, dst, to, sem):
            return pltpu.make_async_remote_copy(
                src_ref=src,
                dst_ref=dst,
                send_sem=gather_send.at[base + sem],
                recv_sem=gather_recv.at[base + sem],
                device_id=(band, to),
                device_id_type=MESH,
            )

        mine = rows(sub, 0, each)
        own = pltpu.make_async_copy(value, mine, out_sem.at[base // 4])
        first = [remote(value, mine, right, 0), remote(value, mine, left, 1)]
        half = each // 2
        a, b = rows(left, 0, half), rows(right, half, half)
        second = [remote(a, a, right, 2), remote(b, b, left, 3)]

        def start():
            own.start()
            for copy in first:
                copy.start()

        def forward():
            for n in range(2):
                first[n].wait_recv()
                second[n].start()

        def finish():
            own.wait()
            for copy in first:
                copy.wait_send()
            for copy in second:
                copy.wait_send()
                copy.wait_recv()

        return start, forward, finish

    ring_one, ring_two = ring(one_v, one_ref, 32, 0), ring(two_v, two_ref, 16, 4)

    arrive(s4, r4, 2, 19)
    coarse(2, T["c1"], u1, 32, 8)

    def radix_one(step, _):
        out = grid_values(u1, u1, T["tw1"], step, pl.ds(0, 128), pl.ds(128, 128), 4)
        for q in range(32):
            one_v[rows8(step), pl.ds(128 * q, 128)] = out[q]
        return 0

    lax.fori_loop(0, 4, radix_one, 0)
    ring_one[0]()

    arrive(s4, r4, 4, 21, 2)
    coarse(4, T["c2"], u2, 16, 2)

    def radix_two(step, _):
        out = grid_values(u2, u2, T["tw2"], step, pl.ds(0, 64), pl.ds(64, 64), 2)
        for q in range(16):
            two_v[rows8(step), pl.ds(128 * q, 128)] = jnp.concatenate([out[2 * q], out[2 * q + 1]], axis=1)
        return 0

    lax.fori_loop(0, 2, radix_two, 0)
    ring_two[0]()

    arrive(s4, r4, 0, 17)
    arrive(s4, r4, 1, 18)
    u0, u0p = u4.at[0], up.at[0]

    def section_first(step, _):
        parts = [[transposed(m, 2 * step + g) for m in range(2)] for g in range(2)]
        both = [
            jnp.concatenate([jnp.concatenate([parts[g][0][j], parts[g][1][j]], axis=1) for g in range(2)], axis=0)
            for j in range(2)
        ]
        u0[pl.ds(pl.multiple_of(step * 256, 256), 256), :] = three(both, T["e8"][0, 0], T["e8"][1, 0])
        return 0

    lax.fori_loop(0, 4, section_first, 0)
    parts = [transposed(m, 0) for m in range(2)]
    both = [jnp.concatenate([parts[0][j][:64], parts[1][j][:64]], axis=1) for j in range(2)]
    u0p[...] = three(both, T["e8"][0, 1], T["e8"][1, 1])
    ring_one[1]()
    ring_two[1]()

    arrive(s4, r4, 3, 20, 6)

    def section_last(step, _):
        a = [transposed(3, 2 * step + g, 6) for g in range(2)]
        both = [jnp.concatenate([a[0][j], a[1][j]], axis=0) for j in range(2)]
        to = pl.ds(pl.multiple_of(step * 256, 256), 256)
        u0[to, :] = u0[to, :] + three(both, T["e3"][0, 0], T["e3"][1, 0])
        return 0

    lax.fori_loop(0, 4, section_last, 0)
    a = transposed(3, 0, 6)
    u0p[...] = u0p[...] + three((a[0][:64], a[1][:64]), T["e3"][0, 1], T["e3"][1, 1])

    def radix_section(step, _):
        for h in range(2):
            lanes, ims = pl.ds(128 * h, 128), pl.ds(256 + 128 * h, 128)
            out = grid_values(u0, u0p, T["tw"], step, lanes, ims, 8)
            for q in range(32):
                x_v[rows8(step), pl.ds(256 * q + 128 * h, 128)] = out[q]
        return 0

    lax.fori_loop(0, 8, radix_section, 0)
    final = pltpu.make_async_copy(x_v, section_ref, out_sem.at[2])
    final.start()
    for m in range(3):
        whole(s1, r1, m, m, 8 if m < 2 else 6).wait_send()
        whole(s3, r3, m, 14 + m, 8 if m < 2 else 6).wait_send()
    for i in range(11):
        whole(s2, r2, i, 3 + i).wait_send()
    for m, each in enumerate((8, 8, 8, 6, 2)):
        whole(s4, r4, m, 17 + m, each).wait_send()
    ring_one[2]()
    ring_two[2]()
    final.wait()


def split_n(x, pieces):
    out = []
    for _ in range(pieces):
        out.append(x.astype(bf16))
        x = x - out[-1].astype(f32)
    return out


def wave_y():
    k = lax.broadcasted_iota(jnp.int32, (128, 128), 0)
    lane = lax.broadcasted_iota(jnp.int32, (128, 128), 1)
    j = lane % 64
    return k + 128 * jnp.where(j < 32, j, j - 64)


def column_backward(fields, tc_ref, bo_ref, qb_table):
    stacked = jnp.concatenate(fields, axis=0) if len(fields) > 1 else fields[0]
    u = dot_right(stacked, qb_table)
    c, s = tc_ref[0], tc_ref[1]
    cols = []
    for n in range(len(fields)):
        r, im = u[128 * n : 128 * n + 128, :128], u[128 * n : 128 * n + 128, 128:]
        cols.append(jnp.concatenate([r * c - im * s, r * s + im * c], axis=0))
    joined = jnp.concatenate(cols, axis=1) if len(cols) > 1 else cols[0]
    out = dot_left(pair(bo_ref), joined)
    return [out[:, 128 * n : 128 * n + 128] for n in range(len(fields))]


def all_tables():
    fg, fs = forward_row_tables()
    g8, g3 = backward_field_tables()
    e8, e3, c1, c2 = backward_next_tables()
    outer = column_outer()
    inner = column_inner(64, 1, 1)
    return {
        "tw": row_twiddle(N),
        "fg": fg,
        "fs": fs,
        "fo": thirds(outer[0]),
        "tc": column_twiddle(64, 2),
        "qf": thirds(inner.T),
        "bo": halves(outer[1]),
        "qb": halves(inner),
        "g8": g8,
        "g3": g3,
        "tc1": column_twiddle(32, 4),
        "tc2": column_twiddle(16, 8),
        "q1": halves(column_inner(32, 2, 1)),
        "q2": halves(column_inner(16, 4, 1)),
        "e8": e8,
        "e3": e3,
        "c1": c1,
        "c2": c2,
        "tw1": row_twiddle(N // 2),
        "tw2": row_twiddle(N // 4),
    }


def local(vorticity):
    tables = all_tables()
    names = tuple(tables)
    anywhere = pl.BlockSpec(memory_space=pl.ANY)
    shapes = [(64, N), (128, N // 2), (64, N // 4)]
    part = lambda n: (n, 8 * DEV, 128)
    scratch = [(64, N), (1024, 512), part(3), part(3), part(11), part(11), (4, 1024, 512), (4, 64, 512)]
    scratch += [part(3), part(3), part(5), part(5), (12, 128, 256), (8, 128, 256)]
    scratch += [(32, N // 2), (16, N // 4), (512, 256), (256, 128)]
    dma = pltpu.SemaphoreType.DMA
    section, one, two = pl.pallas_call(
        functools.partial(kernel, names),
        out_shape=[jax.ShapeDtypeStruct(s, f32) for s in shapes],
        in_specs=[anywhere] * (1 + len(names)),
        out_specs=[anywhere] * 3,
        scratch_shapes=[pltpu.VMEM(s, f32) for s in scratch]
        + [pltpu.VMEM(t.shape, t.dtype) for t in tables.values()]
        + [dma((22,)), dma((22,)), dma((22,)), dma((len(names) + 1,)), dma((8,)), dma((8,)), dma((3,))],
        compiler_params=pltpu.CompilerParams(
            collective_id=0, has_side_effects=True, vmem_limit_bytes=60 * 2**20
        ),
    )(vorticity, *[jnp.asarray(t) for t in tables.values()])
    return section, one, two


def solution(mesh):
    return jax.shard_map(
        local,
        mesh=mesh,
        in_specs=(P(AXES, None),),
        out_specs=(P(AXES, None), P("band", None), P("band", None)),
        check_vma=False,
    )
```

```python
import functools
import math

import jax
import jax.numpy as jnp
import ml_dtypes
import numpy as np
from jax import lax
from jax.experimental import pallas as pl
from jax.experimental.pallas import tpu as pltpu
from jax.sharding import PartitionSpec as P

time_step = 0.2
viscosity = 0.4
forcing = 1.0
force_waves = 4.0

N = 8192
CUT = N // 3
DEV = 128
AXES = ("band", "sub")
f32 = jnp.float32
bf16 = jnp.bfloat16


def halves(table):
    table = np.asarray(table, np.float64).astype(np.float32)
    high = table.astype(ml_dtypes.bfloat16)
    low = (table - high.astype(np.float32)).astype(ml_dtypes.bfloat16)
    return np.stack([high, low])


def wave_of(t):
    return np.where(t % 2 == 1, -(t + 1) // 2, t // 2)


def slot_index():
    e, i = np.meshgrid(np.arange(16), np.arange(11), indexing="ij")
    return e + 16 * i


def backward_row_values(t, length):
    plen = length // 32
    p = np.arange(plen)
    ang = 2 * np.pi * ((wave_of(t)[..., None] * p) % plen) / plen
    gen = np.zeros(t.shape + (2, 2, plen))
    gen[..., 0, 0, :], gen[..., 1, 0, :] = np.cos(ang), -np.sin(ang)
    gen[..., 0, 1, :], gen[..., 1, 1, :] = np.sin(ang), np.cos(ang)
    ang = 2 * np.pi * ((16 * t[..., None] * p) % length) / length
    odd = (t % 2 == 1)[..., None]
    spe = np.zeros(t.shape + (2, 2, plen))
    spe[..., 0, 0, :], spe[..., 1, 0, :] = np.where(odd, 0, np.cos(ang)), np.where(odd, 0, -np.sin(ang))
    spe[..., 0, 1, :], spe[..., 1, 1, :] = np.where(odd, np.cos(ang), 0), np.where(odd, -np.sin(ang), 0)
    return np.stack([gen, spe]).reshape((2,) + t.shape + (2, 2 * plen))


def thirds(table):
    left = np.asarray(table, np.float64).astype(np.float32)
    out = []
    for _ in range(3):
        out.append(left.astype(ml_dtypes.bfloat16))
        left = left - out[-1].astype(np.float32)
    return np.stack(out)


def stack3(pair_of):
    return np.concatenate([pair_of[0], pair_of[1], pair_of[0]], axis=1)


def forward_row_tables():
    t = slot_index()
    p = np.arange(256)
    out = np.zeros((2, 16, 2, 12, 2, 256))
    ang = 2 * np.pi * ((wave_of(t)[:, :, None] * p) % 256) / 256
    out[0, :, 0, :11, 0], out[0, :, 0, :11, 1] = np.cos(ang), np.sin(ang)
    out[0, :, 1, :11, 0], out[0, :, 1, :11, 1] = -np.sin(ang), np.cos(ang)
    ang = 2 * np.pi * ((16 * t[:, :, None] * p) % N) / N
    odd = (t % 2 == 1)[:, :, None]
    out[1, :, 0, :11, 0], out[1, :, 1, :11, 0] = np.where(odd, 0, np.cos(ang)), np.where(odd, 0, -np.sin(ang))
    out[1, :, 0, :11, 1], out[1, :, 1, :11, 1] = np.where(odd, np.cos(ang), 0), np.where(odd, -np.sin(ang), 0)
    full = np.zeros((2, 3, 16, 8, 512))
    for ri in range(2):
        for i in range(11):
            full[:, i // 4, :, ri * 4 + i % 4 if i < 8 else ri * 3 + i - 8] = out[:, :, ri, i].reshape(2, 16, 512)
    full = np.moveaxis(thirds(full.reshape(2, 384, 512)), 0, 1).reshape(2, 1152, 512)
    return full[0], full[1]


def backward_field_tables():
    v = backward_row_values(slot_index(), N).transpose(0, 3, 2, 1, 4)
    return halves(v[:, :, :8].reshape(2, 256, 512)), stack3(halves(v[:, :, 8:].reshape(2, 96, 512)))


def backward_next_tables():
    t = slot_index()
    v = backward_row_values(t, N)
    full = np.zeros((2, 3, 16, 8, 512))
    for ri in range(2):
        for i in range(11):
            full[:, i // 4, :, ri * 4 + i % 4 if i < 8 else ri * 3 + i - 8] = v[:, :, i, ri]
    v1 = backward_row_values(t, N // 2)
    one = np.zeros((2, 2, 16, 8, 256))
    v2 = backward_row_values(t, N // 4)
    two = np.zeros((2, 4, 16, 8, 128))
    for ri in range(2):
        for i in range(8):
            one[:, i % 2, :, (i // 2) * 2 + ri] = v1[:, :, i, ri]
        for i in range(4):
            two[:, i, :, ri] = v2[:, :, i, ri]
    full = full.reshape(2, 384, 512)
    return (
        halves(full[:, :256]),
        halves(full[:, 256:]),
        halves(one.reshape(2, 256, 256)),
        halves(two.reshape(2, 512, 128)),
    )


def row_twiddle(length):
    plen = length // 32
    ang = 2 * np.pi * np.arange(16)[:, None] * np.arange(plen) / length
    return (0.5 * np.stack([np.cos(ang), np.sin(ang)])).astype(np.float32)


def column_outer():
    ang = 2 * np.pi * ((np.arange(128)[:, None] * np.arange(128)) % 128) / 128
    c, s = np.cos(ang), np.sin(ang)
    return np.block([[c, s], [-s, c]]), np.block([[c, -s], [s, c]])


def column_twiddle(rows_each, copies):
    length = DEV * rows_each
    ang = 2 * np.pi * np.arange(128)[:, None] * np.arange(rows_each) / length
    return np.stack([np.tile(np.cos(ang), (1, copies)), np.tile(np.sin(ang), (1, copies))]).astype(np.float32)


def column_inner(rows_each, copies, sign):
    j = np.arange(64)
    signed = np.where(j < 32, j, j - 64)
    ang = 2 * np.pi * ((signed[:, None] * np.arange(rows_each)) % rows_each) / rows_each
    keep = ((signed >= -rows_each // 2) & (signed < rows_each // 2))[:, None]
    c, s = np.cos(ang) * keep, np.sin(ang) * keep
    out = np.zeros((copies, 2, 2, 64, 2, copies, 2, rows_each))
    for m in range(copies):
        for k in range(2):
            out[m, 0, k, :, 0, m, k], out[m, 1, k, :, 0, m, k] = c, -s
            out[m, 0, k, :, 1, m, k], out[m, 1, k, :, 1, m, k] = s, c
    return out.reshape(copies * 256, 2 * copies * 2 * rows_each)


def cmul_const(a, ang):
    r, i = a
    n = round(ang / (math.pi / 16)) % 32
    if n == 0:
        return (r, i)
    if n == 8:
        return (-i, r)
    if n == 16:
        return (-r, -i)
    if n == 24:
        return (i, -r)
    h = math.sqrt(0.5)
    if n == 4:
        return ((r - i) * h, (r + i) * h)
    if n == 12:
        return ((r + i) * (-h), (r - i) * h)
    if n == 20:
        return ((i - r) * h, (r + i) * (-h))
    if n == 28:
        return ((r + i) * h, (i - r) * h)
    c, s = math.cos(n * math.pi / 16), math.sin(n * math.pi / 16)
    return (r * c - i * s, r * s + i * c)


def cadd(a, b):
    return (a[0] + b[0], a[1] + b[1])


def csub(a, b):
    return (a[0] - b[0], a[1] - b[1])


def fft_small(z, sign):
    n = len(z)
    if n == 1:
        return z
    if n == 2:
        return [cadd(z[0], z[1]), csub(z[0], z[1])]
    even, odd = fft_small(z[0::2], sign), fft_small(z[1::2], sign)
    out = [None] * n
    for k in range(n // 2):
        w = cmul_const(odd[k], sign * 2 * math.pi * k / n)
        out[k], out[k + n // 2] = cadd(even[k], w), csub(even[k], w)
    return out


def forward32(x):
    z = fft_small([(x[2 * m], x[2 * m + 1]) for m in range(16)], -1)
    ends = (z[0][0] + z[0][1], z[0][0] - z[0][1])
    rest = [None] * 16
    for k in range(1, 9):
        a, b = z[k], z[16 - k]
        even = (a[0] + b[0], a[1] - b[1])
        odd = (a[1] + b[1], b[0] - a[0])
        turned = cmul_const(odd, -2 * math.pi * k / 32)
        rest[k] = cadd(even, turned)
        if k < 8:
            other = csub(even, turned)
            rest[16 - k] = (other[0], -other[1])
    return ends, rest


def backward32(ends, rest):
    z = [None] * 16
    z[0] = (ends[0] + ends[1], ends[0] - ends[1])
    for k in range(1, 9):
        a, b = rest[k], rest[16 - k]
        even = (a[0] + b[0], a[1] - b[1])
        odd = cmul_const((a[0] - b[0], a[1] + b[1]), 2 * math.pi * k / 32)
        z[k] = (even[0] - odd[1], even[1] + odd[0])
        if k < 8:
            z[16 - k] = (even[0] + odd[1], odd[0] - even[1])
    z = fft_small(z, 1)
    out = []
    for m in range(16):
        out += [z[m][0], z[m][1]]
    return out


def split(x):
    high = x.astype(bf16)
    low = (x - high.astype(f32)).astype(bf16)
    return high, low


def mm(a, b, dims):
    return lax.dot_general(a, b, (dims, ((), ())), preferred_element_type=f32)


def dot_right(x, table, dims=((1,), (0,))):
    high, low = split(x)
    return mm(high, table[0], dims) + (mm(high, table[1], dims) + mm(low, table[0], dims))


def dot_left(table, x, dims=((1,), (0,))):
    high, low = split(x)
    return mm(table[0], high, dims) + (mm(table[0], low, dims) + mm(table[1], high, dims))


def pair(ref, *lead):
    return ref[(0,) + lead], ref[(1,) + lead]


MESH = pl.DeviceIdType.MESH
half_step = 0.5 * time_step
NN = ((1,), (0,))


def rows8(n):
    return pl.ds(pl.multiple_of(n * 8, 8), 8)


def kernel(names, *refs):
    count = len(names)
    ins, rest = refs[: count + 1], refs[count + 1 :]
    x_hbm, table_hbm = ins[0], ins[1:]
    section_ref, one_ref, two_ref = rest[:3]
    (x_v, y_ref, s1, r1, s2, r2, u4, up, s3, r3, s4, r4, vort_ref, next_ref, one_v, two_v, u1, u2) = rest[3:21]
    tables = rest[21 : 21 + count]
    send_sem, recv_sem, own_sem, load_sem, gather_send, gather_recv, out_sem = rest[21 + count :]
    T = dict(zip(names, tables))

    band, sub = lax.axis_index("band"), lax.axis_index("sub")
    me = band * 4 + sub
    y, z, c = band // 8, (band // 2) % 4, band % 2

    def wrap(v):
        return jnp.where(v >= 4, v - 4, v)

    xs, cs = [sub] + [wrap(sub + k) for k in range(1, 4)], [c, 1 - c]

    def each_peer(act, first=0, last=16):
        def group(dy, dz, skip):
            for k in range(4):
                base = (wrap(wrap(y + dy) + k) * 4 + wrap(wrap(z + dz) + k)) * 2
                for d in range(2):
                    if not (skip and k == 0 and d == 0):
                        act(base + cs[d], xs[k])

        if first == 0:
            group(0, 0, True)

        def body(w, _):
            dy = w // 4
            group(dy, w - 4 * dy, False)
            return 0

        lax.fori_loop(max(first, 1), last, body, 0)

    def load(n):
        if n < 0:
            return pltpu.make_async_copy(x_hbm, x_v, load_sem.at[count])
        return pltpu.make_async_copy(table_hbm[n], tables[n], load_sem.at[n])

    load(-1).start()
    for n in range(count):
        load(n).start()

    barrier = pltpu.get_barrier_semaphore()

    def greet(*to):
        pl.semaphore_signal(barrier, inc=1, device_id=to, device_id_type=MESH)

    each_peer(greet)

    def rows_of(n, count):
        return pl.ds(pl.multiple_of(n * 8, 8), count)

    def send(src, dst, m, sem, each=8):
        own = rows_of(me, each)
        pltpu.make_async_copy(src.at[m, own], dst.at[m, own], own_sem.at[sem]).start()

        def one(*to):
            pltpu.make_async_remote_copy(
                src_ref=src.at[m, rows_of(to[0] * 4 + to[1], each)],
                dst_ref=dst.at[m, own],
                send_sem=send_sem.at[sem],
                recv_sem=recv_sem.at[sem],
                device_id=to,
                device_id_type=MESH,
            ).start()

        each_peer(one)

    def whole(src, dst, m, sem, each=8):
        return pltpu.make_async_remote_copy(
            src_ref=src.at[m, pl.ds(0, each * (DEV - 1))],
            dst_ref=dst.at[m, pl.ds(0, each * (DEV - 1))],
            send_sem=send_sem.at[sem],
            recv_sem=recv_sem.at[sem],
            device_id=(band, xs[1]),
            device_id_type=MESH,
        )

    def arrive(src, dst, m, sem, each=8):
        own = rows_of(me, each)
        pltpu.make_async_copy(src.at[m, own], dst.at[m, own], own_sem.at[sem]).wait()
        whole(src, dst, m, sem, each).wait_recv()

    def put_forward(step, x, lanes, h, rows):
        ends, rest = forward32(x)
        y_ref[rows, pl.ds(128 * h, 128)] = ends[0]
        y_ref[rows, pl.ds(256 + 128 * h, 128)] = ends[1]
        tw = T["tw"]
        for k in range(1, 16):
            cs, sn = tw[0, k : k + 1, lanes], tw[1, k : k + 1, lanes]
            r, i = rest[k]
            to = rows8(k * 8 + step)
            y_ref[to, pl.ds(128 * h, 128)] = r * cs + i * sn
            y_ref[to, pl.ds(256 + 128 * h, 128)] = i * cs - r * sn

    def row_products(s, r, base, pieces, ready):
        def value(table, v):
            total = None
            for n, part in enumerate(split_n(v, pieces)):
                out = mm(table[: 384 * (pieces - n)], part, ((1,), (1,)))
                for k in range(pieces - n):
                    one = out[384 * k : 384 * k + 384]
                    total = one if total is None else total + one
            return total

        def product(step, _):
            out = value(T["fg"], y_ref[pl.ds(pl.multiple_of(step * 256, 256), 256), :])
            for g in range(2):
                to = pl.ds(pl.multiple_of((2 * step + g) * 128, 128), 128)
                for m in range(3):
                    s[m, to, :] = out[128 * m : 128 * m + 128, 128 * g : 128 * g + 128]
            return 0

        lax.fori_loop(0, 4, product, 0)
        tail = value(T["fs"], y_ref[:64, :])
        for m in range(3):
            s[m, :128, :64] = tail[128 * m : 128 * m + 128]
        ready()
        for m in range(3):
            send(s, r, m, base + m, 8 if m < 2 else 6)

    load(-1).wait()
    load(0).wait()

    def radix_first(step, _):
        rows = rows8(step)
        for h in range(2):
            x = [x_v[rows, pl.ds(256 * q + 128 * h, 128)] for q in range(32)]
            put_forward(step, x, pl.ds(128 * h, 128), h, rows)
        return 0

    lax.fori_loop(0, 8, radix_first, 0)
    load(1).wait()
    load(2).wait()
    row_products(s1, r1, 0, 3, lambda: pl.semaphore_wait(barrier, DEV - 1))
    for n in range(3, count):
        load(n).wait()

    ky = wave_y()
    factor = 2.0 * math.pi / N
    kappa_y = factor * ky.astype(f32)
    kept_y = (jnp.abs(ky) <= CUT).astype(f32)

    def forward_four(r, m, pieces):
        blocks, four = [], 4 if m < 2 else 3
        for ii in range(four):
            both = [r[m, pl.ds(ri * four + ii, 128, stride=8), :] for ri in range(2)]
            blocks.append(jnp.concatenate(both, axis=0))
        parts = split_n(jnp.concatenate(blocks, axis=1), pieces)
        out = sum(mm(T["fo"][k], parts[n], NN) for n in range(pieces) for k in range(pieces - n))
        cs, sn = T["tc"][0], T["tc"][1]
        turned = []
        for ii in range(four):
            re, im = out[:128, 128 * ii : 128 * ii + 128], out[128:, 128 * ii : 128 * ii + 128]
            turned.append(jnp.concatenate([re * cs + im * sn, im * cs - re * sn], axis=1))
        parts = split_n(jnp.concatenate(turned, axis=0), pieces)
        out = sum(mm(parts[n], T["qf"][k], NN) for n in range(pieces) for k in range(pieces - n))
        return [(out[128 * ii : 128 * ii + 128, :128], out[128 * ii : 128 * ii + 128, 128:]) for ii in range(four)]

    def x_part(i):
        g, e = me // 16, me % 16
        t = e + 16 * i
        lane = lax.broadcasted_iota(jnp.int32, (1, 128), 1)
        k2 = 2 * g + lane // 64
        j2 = jnp.where(t % 2 == 1, -((t + 1) // 2), t // 2)
        kx = jnp.where(k2 == 0, 16 * t, k2 + 32 * j2)
        kappa_x = factor * kx.astype(f32)
        weight = jnp.where(kx == 0, 1.0, 2.0) / (float(N) * float(N))
        return kappa_x, (jnp.abs(kx) <= CUT).astype(f32), weight

    for m in range(3):
        arrive(s1, r1, m, m, 8 if m < 2 else 6)
        four = forward_four(r1, m, 3)
        for ii in range(len(four)):
            vort_ref[4 * m + ii, :, :128], vort_ref[4 * m + ii, :, 128:] = four[ii]

        def slot(i, _):
            kappa_x, kept_x, weight = x_part(i)
            kept = kept_y * kept_x
            kappa_sq = kappa_x * kappa_x + kappa_y * kappa_y
            vr, vi = vort_ref[i, :, :128] * kept, vort_ref[i, :, 128:] * kept
            vort_ref[i, :, :128], vort_ref[i, :, 128:] = vr, vi
            positive = kappa_sq > 0
            inverse_sq = jnp.where(positive, 1.0 / jnp.where(positive, kappa_sq, 1.0), 0.0)
            sr, si = vr * inverse_sq, vi * inverse_sq
            kxw, kyw = kappa_x * weight, kappa_y * weight
            fields = [
                jnp.concatenate([-kyw * si, kyw * sr], axis=1),
                jnp.concatenate([kxw * si, -kxw * sr], axis=1),
                jnp.concatenate([-kxw * vi, kxw * vr], axis=1),
                jnp.concatenate([-kyw * vi, kyw * vr], axis=1),
            ]
            outs = column_backward(fields, T["tc"], T["bo"], pair(T["qb"]))
            for f in range(4):
                for ri in range(2):
                    s2[i, pl.ds(f * 2 + ri, 128, stride=8), :] = outs[f][128 * ri : 128 * ri + 128]
            send(s2, r2, i, 3 + i)
            return 0

        lax.fori_loop(4 * m, min(4 * m + 4, 11), slot, 0)

    def gather_rows(f, g, slots):
        parts = []
        for ri in range(2):
            for i in slots:
                parts.append(r2[i, pl.ds(g * 128 + f * 2 + ri, 16, stride=8), :])
        return split(jnp.concatenate(parts, axis=0))

    def three(a, th, tl):
        return mm(a[0], th, NN) + (mm(a[0], tl, NN) + mm(a[1], th, NN))

    for part, (slots, table) in enumerate(((range(8), "g8"), (range(8, 11), "g3"))):
        for i in slots:
            arrive(s2, r2, i, 3 + i)
        gt = T[table]

        def value(fgs, kind, rows):
            got = [gather_rows(f, g, slots) for f, g in fgs]
            if part == 0:
                both = [jnp.concatenate([a[j].T[:rows] for a in got], axis=0) for j in range(2)]
                return three(both, gt[0, kind], gt[1, kind])
            both = [jnp.concatenate([a[0], a[0], a[1]], axis=0).T[:rows] for a in got]
            return mm(jnp.concatenate(both, axis=0), gt[kind], NN)

        def pairs(n, _):
            f, step = n // 2, n % 2
            out = value([(f, 4 * step + k) for k in range(4)], 0, 128)
            to = pl.ds(pl.multiple_of(step * 512, 512), 512)
            u4[f, to, :] = out if part == 0 else u4[f, to, :] + out
            return 0

        lax.fori_loop(0, 8, pairs, 0)

        edge = value([(f, 0) for f in range(4)], 1, 64)
        for f in range(4):
            out = edge[64 * f : 64 * f + 64]
            up[f] = out if part == 0 else up[f] + out

    def grid_values(u, edge, tw, step, lanes, ims, stride):
        ends = (edge[rows8(step), lanes], edge[rows8(step), ims])
        rest = [None] * 16
        for k in range(1, 16):
            cs, sn = tw[0, k : k + 1, lanes], tw[1, k : k + 1, lanes]
            at = rows8(k * stride + step)
            r, i = u[at, lanes], u[at, ims]
            rest[k] = (r * cs - i * sn, r * sn + i * cs)
        return backward32(ends, rest)

    def radix_product(step, _):
        row = lax.broadcasted_iota(jnp.int32, (8, 128), 0) + (me * 64 + step * 8)
        drive = forcing * jnp.sin((2.0 * math.pi * force_waves / N) * row.astype(f32))
        for h in range(2):
            lanes, ims = pl.ds(128 * h, 128), pl.ds(256 + 128 * h, 128)
            vals = [None] * 4
            for f in (0, 2, 1, 3):
                vals[f] = grid_values(u4.at[f], up.at[f], T["tw"], step, lanes, ims, 8)
                if f == 2:
                    total = [vals[0][q] * vals[2][q] for q in range(32)]
            x = [total[q] + vals[1][q] * vals[3][q] - drive for q in range(32)]
            put_forward(step, x, lanes, h, rows8(step))
        return 0

    lax.fori_loop(0, 8, radix_product, 0)
    row_products(s3, r3, 14, 2, lambda: None)

    inside_one = jnp.concatenate([(jnp.abs(ky) < 2048).astype(f32)] * 2, axis=1)
    inside_two = jnp.concatenate([(jnp.abs(ky) < 1024).astype(f32)] * 2, axis=1)

    def whole_blocks(m, blocks):
        outs = column_backward(blocks, T["tc"], T["bo"], pair(T["qb"]))
        for ii, out in enumerate(outs):
            for ri in range(2):
                to, r = (m, ri * 4 + ii) if m < 2 else (3, ri * 3 + ii)
                s4[to, pl.ds(r, 128, stride=8), :] = out[128 * ri : 128 * ri + 128]

    for m in range(3):
        arrive(s3, r3, m, 14 + m, 8 if m < 2 else 6)
        blocks = []
        for ii, (ar, ai) in enumerate(forward_four(r3, m, 2)):
            i = 4 * m + ii
            kappa_x, kept_x, weight = x_part(i)
            kept = kept_y * kept_x
            kappa_sq = kappa_x * kappa_x + kappa_y * kappa_y
            vr, vi = vort_ref[i, :, :128], vort_ref[i, :, 128:]
            ar, ai = ar * kept, ai * kept
            nr = (vr + half_step * (-ar - viscosity * kappa_sq * vr)) * weight
            ni = (vi + half_step * (-ai - viscosity * kappa_sq * vi)) * weight
            blocks.append(jnp.concatenate([nr, ni], axis=1))
            if i < 8:
                next_ref[i] = blocks[-1]
        if m == 0:
            whole_blocks(0, blocks)
            send(s4, r4, 0, 17)
        if m == 1:
            pairs_of = [
                jnp.concatenate([next_ref[2 * n] * inside_one, next_ref[2 * n + 1] * inside_one], axis=1)
                for n in range(4)
            ]
            for n, out in enumerate(column_backward(pairs_of, T["tc1"], T["bo"], pair(T["q1"]))):
                for ri in range(2):
                    s4[2, pl.ds(2 * n + ri, 128, stride=8), :] = out[128 * ri : 128 * ri + 128]
            send(s4, r4, 2, 19)
            block = jnp.concatenate([next_ref[n] * inside_two for n in range(4)], axis=1)
            (out,) = column_backward([block], T["tc2"], T["bo"], pair(T["q2"]))
            for ri in range(2):
                s4[4, pl.ds(ri, 128, stride=8), :] = out[128 * ri : 128 * ri + 128]
            send(s4, r4, 4, 21, 2)
            whole_blocks(1, blocks)
            send(s4, r4, 1, 18)
        if m == 2:
            whole_blocks(2, blocks)
            send(s4, r4, 3, 20, 6)

    def transposed(m, g, valid=8):
        block = r4[m, pl.ds(pl.multiple_of(g * 128, 128), 128), :]
        if valid < 8:
            row = lax.broadcasted_iota(jnp.int32, (128, 128), 0) % 8
            block = jnp.where(row < valid, block, 0.0)
        high, low = split(block)
        return high.T, low.T

    def coarse(m, table, u, each, valid):
        copies = 64 // each

        def value(gs, kind):
            both = [[], []]
            for g in gs:
                a = transposed(m, g, valid)
                for j in range(2):
                    parts = [a[j][n * 2 * each : (n + 1) * 2 * each] for n in range(copies)]
                    both[j].append(jnp.concatenate(parts, axis=1))
            both = [jnp.concatenate(v, axis=0) for v in both]
            return three(both, table[0, kind], table[1, kind])

        def product(n, _):
            out = value([4 * n + k for k in range(4)], 0)
            u[pl.ds(pl.multiple_of(n * 8 * each, 8 * each), 8 * each), :] = out
            return 0

        lax.fori_loop(0, 2, product, 0)
        u[:each, :] = value([0], 1)[:each]

    right, left = (sub + 1) % 4, (sub + 3) % 4

    def ring(value, out, each, base):
        def rows(owner, start, size):
            return out.at[pl.ds(pl.multiple_of(owner * each + start, 8), size)]

        def remote(src, dst, to, sem):
            return pltpu.make_async_remote_copy(
                src_ref=src,
                dst_ref=dst,
                send_sem=gather_send.at[base + sem],
                recv_sem=gather_recv.at[base + sem],
                device_id=(band, to),
                device_id_type=MESH,
            )

        mine = rows(sub, 0, each)
        own = pltpu.make_async_copy(value, mine, out_sem.at[base // 4])
        first = [remote(value, mine, right, 0), remote(value, mine, left, 1)]
        half = each // 2
        a, b = rows(left, 0, half), rows(right, half, half)
        second = [remote(a, a, right, 2), remote(b, b, left, 3)]

        def start():
            own.start()
            for copy in first:
                copy.start()

        def forward():
            for n in range(2):
                first[n].wait_recv()
                second[n].start()

        def finish():
            own.wait()
            for copy in first:
                copy.wait_send()
            for copy in second:
                copy.wait_send()
                copy.wait_recv()

        return start, forward, finish

    ring_one, ring_two = ring(one_v, one_ref, 32, 0), ring(two_v, two_ref, 16, 4)

    arrive(s4, r4, 2, 19)
    coarse(2, T["c1"], u1, 32, 8)

    def radix_one(step, _):
        out = grid_values(u1, u1, T["tw1"], step, pl.ds(0, 128), pl.ds(128, 128), 4)
        for q in range(32):
            one_v[rows8(step), pl.ds(128 * q, 128)] = out[q]
        return 0

    lax.fori_loop(0, 4, radix_one, 0)
    ring_one[0]()

    arrive(s4, r4, 4, 21, 2)
    coarse(4, T["c2"], u2, 16, 2)

    def radix_two(step, _):
        out = grid_values(u2, u2, T["tw2"], step, pl.ds(0, 64), pl.ds(64, 64), 2)
        for q in range(16):
            two_v[rows8(step), pl.ds(128 * q, 128)] = jnp.concatenate([out[2 * q], out[2 * q + 1]], axis=1)
        return 0

    lax.fori_loop(0, 2, radix_two, 0)
    ring_two[0]()

    arrive(s4, r4, 0, 17)
    arrive(s4, r4, 1, 18)
    u0, u0p = u4.at[0], up.at[0]

    def section_first(step, _):
        parts = [[transposed(m, 4 * step + g) for m in range(2)] for g in range(4)]
        both = [
            jnp.concatenate([jnp.concatenate([parts[g][0][j], parts[g][1][j]], axis=1) for g in range(4)], axis=0)
            for j in range(2)
        ]
        u0[pl.ds(pl.multiple_of(step * 512, 512), 512), :] = three(both, T["e8"][0, 0], T["e8"][1, 0])
        return 0

    lax.fori_loop(0, 2, section_first, 0)
    parts = [transposed(m, 0) for m in range(2)]
    both = [jnp.concatenate([parts[0][j][:64], parts[1][j][:64]], axis=1) for j in range(2)]
    u0p[...] = three(both, T["e8"][0, 1], T["e8"][1, 1])
    ring_one[1]()
    ring_two[1]()

    arrive(s4, r4, 3, 20, 6)

    def section_last(step, _):
        a = [transposed(3, 4 * step + g, 6) for g in range(4)]
        both = [jnp.concatenate([v[j] for v in a], axis=0) for j in range(2)]
        to = pl.ds(pl.multiple_of(step * 512, 512), 512)
        u0[to, :] = u0[to, :] + three(both, T["e3"][0, 0], T["e3"][1, 0])
        return 0

    lax.fori_loop(0, 2, section_last, 0)
    a = transposed(3, 0, 6)
    u0p[...] = u0p[...] + three((a[0][:64], a[1][:64]), T["e3"][0, 1], T["e3"][1, 1])

    def radix_section(step, _):
        for h in range(2):
            lanes, ims = pl.ds(128 * h, 128), pl.ds(256 + 128 * h, 128)
            out = grid_values(u0, u0p, T["tw"], step, lanes, ims, 8)
            for q in range(32):
                x_v[rows8(step), pl.ds(256 * q + 128 * h, 128)] = out[q]
        return 0

    lax.fori_loop(0, 8, radix_section, 0)
    final = pltpu.make_async_copy(x_v, section_ref, out_sem.at[2])
    final.start()
    for m in range(3):
        whole(s1, r1, m, m, 8 if m < 2 else 6).wait_send()
        whole(s3, r3, m, 14 + m, 8 if m < 2 else 6).wait_send()
    for i in range(11):
        whole(s2, r2, i, 3 + i).wait_send()
    for m, each in enumerate((8, 8, 8, 6, 2)):
        whole(s4, r4, m, 17 + m, each).wait_send()
    ring_one[2]()
    ring_two[2]()
    final.wait()


def split_n(x, pieces):
    out = []
    for _ in range(pieces):
        out.append(x.astype(bf16))
        x = x - out[-1].astype(f32)
    return out


def wave_y():
    k = lax.broadcasted_iota(jnp.int32, (128, 128), 0)
    lane = lax.broadcasted_iota(jnp.int32, (128, 128), 1)
    j = lane % 64
    return k + 128 * jnp.where(j < 32, j, j - 64)


def column_backward(fields, tc_ref, bo_ref, qb_table):
    stacked = jnp.concatenate(fields, axis=0) if len(fields) > 1 else fields[0]
    u = dot_right(stacked, qb_table)
    c, s = tc_ref[0], tc_ref[1]
    cols = []
    for n in range(len(fields)):
        r, im = u[128 * n : 128 * n + 128, :128], u[128 * n : 128 * n + 128, 128:]
        cols.append(jnp.concatenate([r * c - im * s, r * s + im * c], axis=0))
    joined = jnp.concatenate(cols, axis=1) if len(cols) > 1 else cols[0]
    out = dot_left(pair(bo_ref), joined)
    return [out[:, 128 * n : 128 * n + 128] for n in range(len(fields))]


def all_tables():
    fg, fs = forward_row_tables()
    g8, g3 = backward_field_tables()
    e8, e3, c1, c2 = backward_next_tables()
    outer = column_outer()
    inner = column_inner(64, 1, 1)
    return {
        "tw": row_twiddle(N),
        "fg": fg,
        "fs": fs,
        "fo": thirds(outer[0]),
        "tc": column_twiddle(64, 2),
        "qf": thirds(inner.T),
        "bo": halves(outer[1]),
        "qb": halves(inner),
        "g8": g8,
        "g3": g3,
        "tc1": column_twiddle(32, 4),
        "tc2": column_twiddle(16, 8),
        "q1": halves(column_inner(32, 2, 1)),
        "q2": halves(column_inner(16, 4, 1)),
        "e8": e8,
        "e3": e3,
        "c1": c1,
        "c2": c2,
        "tw1": row_twiddle(N // 2),
        "tw2": row_twiddle(N // 4),
    }


def local(vorticity):
    tables = all_tables()
    names = tuple(tables)
    anywhere = pl.BlockSpec(memory_space=pl.ANY)
    shapes = [(64, N), (128, N // 2), (64, N // 4)]
    part = lambda n: (n, 8 * DEV, 128)
    scratch = [(64, N), (1024, 512), part(3), part(3), part(11), part(11), (4, 1024, 512), (4, 64, 512)]
    scratch += [part(3), part(3), part(5), part(5), (12, 128, 256), (8, 128, 256)]
    scratch += [(32, N // 2), (16, N // 4), (512, 256), (256, 128)]
    dma = pltpu.SemaphoreType.DMA
    section, one, two = pl.pallas_call(
        functools.partial(kernel, names),
        out_shape=[jax.ShapeDtypeStruct(s, f32) for s in shapes],
        in_specs=[anywhere] * (1 + len(names)),
        out_specs=[anywhere] * 3,
        scratch_shapes=[pltpu.VMEM(s, f32) for s in scratch]
        + [pltpu.VMEM(t.shape, t.dtype) for t in tables.values()]
        + [dma((22,)), dma((22,)), dma((22,)), dma((len(names) + 1,)), dma((8,)), dma((8,)), dma((3,))],
        compiler_params=pltpu.CompilerParams(
            collective_id=0, has_side_effects=True, vmem_limit_bytes=60 * 2**20
        ),
    )(vorticity, *[jnp.asarray(t) for t in tables.values()])
    return section, one, two


def solution(mesh):
    return jax.shard_map(
        local,
        mesh=mesh,
        in_specs=(P(AXES, None),),
        out_specs=(P(AXES, None), P("band", None), P("band", None)),
        check_vma=False,
    )
```

```python
import functools
import math

import jax
import jax.numpy as jnp
import ml_dtypes
import numpy as np
from jax import lax
from jax.experimental import pallas as pl
from jax.experimental.pallas import tpu as pltpu
from jax.sharding import PartitionSpec as P

time_step = 0.2
viscosity = 0.4
forcing = 1.0
force_waves = 4.0

N = 8192
CUT = N // 3
DEV = 128
AXES = ("band", "sub")
f32 = jnp.float32
bf16 = jnp.bfloat16


def halves(table):
    table = np.asarray(table, np.float64).astype(np.float32)
    high = table.astype(ml_dtypes.bfloat16)
    low = (table - high.astype(np.float32)).astype(ml_dtypes.bfloat16)
    return np.stack([high, low])


def wave_of(t):
    return np.where(t % 2 == 1, -(t + 1) // 2, t // 2)


def slot_index():
    e, i = np.meshgrid(np.arange(16), np.arange(11), indexing="ij")
    return e + 16 * i


def backward_row_values(t, length):
    plen = length // 32
    p = np.arange(plen)
    ang = 2 * np.pi * ((wave_of(t)[..., None] * p) % plen) / plen
    gen = np.zeros(t.shape + (2, 2, plen))
    gen[..., 0, 0, :], gen[..., 1, 0, :] = np.cos(ang), -np.sin(ang)
    gen[..., 0, 1, :], gen[..., 1, 1, :] = np.sin(ang), np.cos(ang)
    ang = 2 * np.pi * ((16 * t[..., None] * p) % length) / length
    odd = (t % 2 == 1)[..., None]
    spe = np.zeros(t.shape + (2, 2, plen))
    spe[..., 0, 0, :], spe[..., 1, 0, :] = np.where(odd, 0, np.cos(ang)), np.where(odd, 0, -np.sin(ang))
    spe[..., 0, 1, :], spe[..., 1, 1, :] = np.where(odd, np.cos(ang), 0), np.where(odd, -np.sin(ang), 0)
    return np.stack([gen, spe]).reshape((2,) + t.shape + (2, 2 * plen))


def thirds(table):
    left = np.asarray(table, np.float64).astype(np.float32)
    out = []
    for _ in range(3):
        out.append(left.astype(ml_dtypes.bfloat16))
        left = left - out[-1].astype(np.float32)
    return np.stack(out)


def stack3(pair_of):
    return np.concatenate([pair_of[0], pair_of[1], pair_of[0]], axis=1)


def forward_row_tables():
    t = slot_index()
    p = np.arange(256)
    out = np.zeros((2, 16, 2, 12, 2, 256))
    ang = 2 * np.pi * ((wave_of(t)[:, :, None] * p) % 256) / 256
    out[0, :, 0, :11, 0], out[0, :, 0, :11, 1] = np.cos(ang), np.sin(ang)
    out[0, :, 1, :11, 0], out[0, :, 1, :11, 1] = -np.sin(ang), np.cos(ang)
    ang = 2 * np.pi * ((16 * t[:, :, None] * p) % N) / N
    odd = (t % 2 == 1)[:, :, None]
    out[1, :, 0, :11, 0], out[1, :, 1, :11, 0] = np.where(odd, 0, np.cos(ang)), np.where(odd, 0, -np.sin(ang))
    out[1, :, 0, :11, 1], out[1, :, 1, :11, 1] = np.where(odd, np.cos(ang), 0), np.where(odd, -np.sin(ang), 0)
    full = np.zeros((2, 3, 16, 8, 512))
    for ri in range(2):
        for i in range(11):
            full[:, i // 4, :, ri * 4 + i % 4 if i < 8 else ri * 3 + i - 8] = out[:, :, ri, i].reshape(2, 16, 512)
    full = np.moveaxis(thirds(full.reshape(2, 384, 512)), 0, 1)
    full = [full[:, :, :128].reshape(2, 384, 512), full[:, :, 128:].reshape(2, 768, 512)]
    full = np.concatenate(full, axis=1)
    return full[0], full[1]


def backward_field_tables():
    v = backward_row_values(slot_index(), N).transpose(0, 3, 2, 1, 4)
    return halves(v[:, :, :8].reshape(2, 256, 512)), stack3(halves(v[:, :, 8:].reshape(2, 96, 512)))


def backward_next_tables():
    t = slot_index()
    v = backward_row_values(t, N)
    full = np.zeros((2, 3, 16, 8, 512))
    for ri in range(2):
        for i in range(11):
            full[:, i // 4, :, ri * 4 + i % 4 if i < 8 else ri * 3 + i - 8] = v[:, :, i, ri]
    v1 = backward_row_values(t, N // 2)
    one = np.zeros((2, 2, 16, 8, 256))
    v2 = backward_row_values(t, N // 4)
    two = np.zeros((2, 4, 16, 8, 128))
    for ri in range(2):
        for i in range(8):
            one[:, i % 2, :, (i // 2) * 2 + ri] = v1[:, :, i, ri]
        for i in range(4):
            two[:, i, :, ri] = v2[:, :, i, ri]
    full = full.reshape(2, 384, 512)
    return (
        halves(full[:, :256]),
        halves(full[:, 256:]),
        halves(one.reshape(2, 256, 256)),
        halves(two.reshape(2, 512, 128)),
    )


def row_twiddle(length):
    plen = length // 32
    ang = 2 * np.pi * np.arange(16)[:, None] * np.arange(plen) / length
    return (0.5 * np.stack([np.cos(ang), np.sin(ang)])).astype(np.float32)


def column_outer():
    ang = 2 * np.pi * ((np.arange(128)[:, None] * np.arange(128)) % 128) / 128
    c, s = np.cos(ang), np.sin(ang)
    return np.block([[c, s], [-s, c]]), np.block([[c, -s], [s, c]])


def column_twiddle(rows_each, copies):
    length = DEV * rows_each
    ang = 2 * np.pi * np.arange(128)[:, None] * np.arange(rows_each) / length
    return np.stack([np.tile(np.cos(ang), (1, copies)), np.tile(np.sin(ang), (1, copies))]).astype(np.float32)


def column_inner(rows_each, copies, sign):
    j = np.arange(64)
    signed = np.where(j < 32, j, j - 64)
    ang = 2 * np.pi * ((signed[:, None] * np.arange(rows_each)) % rows_each) / rows_each
    keep = ((signed >= -rows_each // 2) & (signed < rows_each // 2))[:, None]
    c, s = np.cos(ang) * keep, np.sin(ang) * keep
    out = np.zeros((copies, 2, 2, 64, 2, copies, 2, rows_each))
    for m in range(copies):
        for k in range(2):
            out[m, 0, k, :, 0, m, k], out[m, 1, k, :, 0, m, k] = c, -s
            out[m, 0, k, :, 1, m, k], out[m, 1, k, :, 1, m, k] = s, c
    return out.reshape(copies * 256, 2 * copies * 2 * rows_each)


def cmul_const(a, ang):
    r, i = a
    n = round(ang / (math.pi / 16)) % 32
    if n == 0:
        return (r, i)
    if n == 8:
        return (-i, r)
    if n == 16:
        return (-r, -i)
    if n == 24:
        return (i, -r)
    h = math.sqrt(0.5)
    if n == 4:
        return ((r - i) * h, (r + i) * h)
    if n == 12:
        return ((r + i) * (-h), (r - i) * h)
    if n == 20:
        return ((i - r) * h, (r + i) * (-h))
    if n == 28:
        return ((r + i) * h, (i - r) * h)
    c, s = math.cos(n * math.pi / 16), math.sin(n * math.pi / 16)
    return (r * c - i * s, r * s + i * c)


def cadd(a, b):
    return (a[0] + b[0], a[1] + b[1])


def csub(a, b):
    return (a[0] - b[0], a[1] - b[1])


def fft_small(z, sign):
    n = len(z)
    if n == 1:
        return z
    if n == 2:
        return [cadd(z[0], z[1]), csub(z[0], z[1])]
    even, odd = fft_small(z[0::2], sign), fft_small(z[1::2], sign)
    out = [None] * n
    for k in range(n // 2):
        w = cmul_const(odd[k], sign * 2 * math.pi * k / n)
        out[k], out[k + n // 2] = cadd(even[k], w), csub(even[k], w)
    return out


def forward32(x):
    z = fft_small([(x[2 * m], x[2 * m + 1]) for m in range(16)], -1)
    ends = (z[0][0] + z[0][1], z[0][0] - z[0][1])
    rest = [None] * 16
    for k in range(1, 9):
        a, b = z[k], z[16 - k]
        even = (a[0] + b[0], a[1] - b[1])
        odd = (a[1] + b[1], b[0] - a[0])
        turned = cmul_const(odd, -2 * math.pi * k / 32)
        rest[k] = cadd(even, turned)
        if k < 8:
            other = csub(even, turned)
            rest[16 - k] = (other[0], -other[1])
    return ends, rest


def backward32(ends, rest):
    z = [None] * 16
    z[0] = (ends[0] + ends[1], ends[0] - ends[1])
    for k in range(1, 9):
        a, b = rest[k], rest[16 - k]
        even = (a[0] + b[0], a[1] - b[1])
        odd = cmul_const((a[0] - b[0], a[1] + b[1]), 2 * math.pi * k / 32)
        z[k] = (even[0] - odd[1], even[1] + odd[0])
        if k < 8:
            z[16 - k] = (even[0] + odd[1], odd[0] - even[1])
    z = fft_small(z, 1)
    out = []
    for m in range(16):
        out += [z[m][0], z[m][1]]
    return out


def split(x):
    high = x.astype(bf16)
    low = (x - high.astype(f32)).astype(bf16)
    return high, low


def mm(a, b, dims):
    return lax.dot_general(a, b, (dims, ((), ())), preferred_element_type=f32)


def dot_right(x, table, dims=((1,), (0,))):
    high, low = split(x)
    return mm(high, table[0], dims) + (mm(high, table[1], dims) + mm(low, table[0], dims))


def dot_left(table, x, dims=((1,), (0,))):
    high, low = split(x)
    return mm(table[0], high, dims) + (mm(table[0], low, dims) + mm(table[1], high, dims))


def pair(ref, *lead):
    return ref[(0,) + lead], ref[(1,) + lead]


MESH = pl.DeviceIdType.MESH
half_step = 0.5 * time_step
NN = ((1,), (0,))


def rows8(n):
    return pl.ds(pl.multiple_of(n * 8, 8), 8)


def kernel(names, *refs):
    count = len(names)
    ins, rest = refs[: count + 1], refs[count + 1 :]
    x_hbm, table_hbm = ins[0], ins[1:]
    section_ref, one_ref, two_ref = rest[:3]
    (x_v, y_ref, s1, r1, s2, r2, u4, up, s3, r3, s4, r4, vort_ref, next_ref, one_v, two_v, u1, u2) = rest[3:21]
    tables = rest[21 : 21 + count]
    send_sem, recv_sem, own_sem, load_sem, gather_send, gather_recv, out_sem = rest[21 + count :]
    T = dict(zip(names, tables))

    band, sub = lax.axis_index("band"), lax.axis_index("sub")
    me = band * 4 + sub
    y, z, c = band // 8, (band // 2) % 4, band % 2

    def wrap(v):
        return jnp.where(v >= 4, v - 4, v)

    xs, cs = [sub] + [wrap(sub + k) for k in range(1, 4)], [c, 1 - c]

    def each_peer(act, first=0, last=16):
        def group(dy, dz, skip):
            for k in range(4):
                base = (wrap(wrap(y + dy) + k) * 4 + wrap(wrap(z + dz) + k)) * 2
                for d in range(2):
                    if not (skip and k == 0 and d == 0):
                        act(base + cs[d], xs[k])

        if first == 0:
            group(0, 0, True)

        def body(w, _):
            dy = w // 4
            group(dy, w - 4 * dy, False)
            return 0

        lax.fori_loop(max(first, 1), last, body, 0)

    def load(n):
        if n < 0:
            return pltpu.make_async_copy(x_hbm, x_v, load_sem.at[count])
        return pltpu.make_async_copy(table_hbm[n], tables[n], load_sem.at[n])

    load(-1).start()
    for n in range(count):
        load(n).start()

    barrier = pltpu.get_barrier_semaphore()

    def greet(*to):
        pl.semaphore_signal(barrier, inc=1, device_id=to, device_id_type=MESH)

    each_peer(greet)

    def rows_of(n, count):
        return pl.ds(pl.multiple_of(n * 8, 8), count)

    def send(src, dst, m, sem, each=8):
        own = rows_of(me, each)
        pltpu.make_async_copy(src.at[m, own], dst.at[m, own], own_sem.at[sem]).start()

        def one(*to):
            pltpu.make_async_remote_copy(
                src_ref=src.at[m, rows_of(to[0] * 4 + to[1], each)],
                dst_ref=dst.at[m, own],
                send_sem=send_sem.at[sem],
                recv_sem=recv_sem.at[sem],
                device_id=to,
                device_id_type=MESH,
            ).start()

        each_peer(one)

    def whole(src, dst, m, sem, each=8):
        return pltpu.make_async_remote_copy(
            src_ref=src.at[m, pl.ds(0, each * (DEV - 1))],
            dst_ref=dst.at[m, pl.ds(0, each * (DEV - 1))],
            send_sem=send_sem.at[sem],
            recv_sem=recv_sem.at[sem],
            device_id=(band, xs[1]),
            device_id_type=MESH,
        )

    def arrive(src, dst, m, sem, each=8):
        own = rows_of(me, each)
        pltpu.make_async_copy(src.at[m, own], dst.at[m, own], own_sem.at[sem]).wait()
        whole(src, dst, m, sem, each).wait_recv()

    def put_forward(step, x, lanes, h, rows):
        ends, rest = forward32(x)
        y_ref[rows, pl.ds(128 * h, 128)] = ends[0]
        y_ref[rows, pl.ds(256 + 128 * h, 128)] = ends[1]
        tw = T["tw"]
        for k in range(1, 16):
            cs, sn = tw[0, k : k + 1, lanes], tw[1, k : k + 1, lanes]
            r, i = rest[k]
            to = rows8(k * 8 + step)
            y_ref[to, pl.ds(128 * h, 128)] = r * cs + i * sn
            y_ref[to, pl.ds(256 + 128 * h, 128)] = i * cs - r * sn

    def row_products(s, r, base, pieces, ready):
        for start, size, ms in ((0, 128, (0,)), (384, 256, (1, 2))):

            def value(table, v):
                total = None
                for n, part in enumerate(split_n(v, pieces)):
                    out = mm(table[start : start + size * (pieces - n)], part, ((1,), (1,)))
                    for k in range(pieces - n):
                        one = out[size * k : size * k + size]
                        total = one if total is None else total + one
                return total

            def product(step, _):
                out = value(T["fg"], y_ref[pl.ds(pl.multiple_of(step * 256, 256), 256), :])
                for g in range(2):
                    to = pl.ds(pl.multiple_of((2 * step + g) * 128, 128), 128)
                    for n, m in enumerate(ms):
                        s[m, to, :] = out[128 * n : 128 * n + 128, 128 * g : 128 * g + 128]
                return 0

            lax.fori_loop(0, 4, product, 0)
            tail = value(T["fs"], y_ref[:64, :])
            for n, m in enumerate(ms):
                s[m, :128, :64] = tail[128 * n : 128 * n + 128]
            if start == 0:
                ready()
            for m in ms:
                send(s, r, m, base + m, 8 if m < 2 else 6)

    load(-1).wait()
    load(0).wait()

    def radix_first(step, _):
        rows = rows8(step)
        for h in range(2):
            x = [x_v[rows, pl.ds(256 * q + 128 * h, 128)] for q in range(32)]
            put_forward(step, x, pl.ds(128 * h, 128), h, rows)
        return 0

    lax.fori_loop(0, 8, radix_first, 0)
    load(1).wait()
    load(2).wait()
    row_products(s1, r1, 0, 3, lambda: pl.semaphore_wait(barrier, DEV - 1))
    for n in range(3, count):
        load(n).wait()

    ky = wave_y()
    factor = 2.0 * math.pi / N
    kappa_y = factor * ky.astype(f32)
    kept_y = (jnp.abs(ky) <= CUT).astype(f32)

    def forward_four(r, m, pieces):
        blocks, four = [], 4 if m < 2 else 3
        for ii in range(four):
            both = [r[m, pl.ds(ri * four + ii, 128, stride=8), :] for ri in range(2)]
            blocks.append(jnp.concatenate(both, axis=0))
        parts = split_n(jnp.concatenate(blocks, axis=1), pieces)
        out = sum(mm(T["fo"][k], parts[n], NN) for n in range(pieces) for k in range(pieces - n))
        cs, sn = T["tc"][0], T["tc"][1]
        turned = []
        for ii in range(four):
            re, im = out[:128, 128 * ii : 128 * ii + 128], out[128:, 128 * ii : 128 * ii + 128]
            turned.append(jnp.concatenate([re * cs + im * sn, im * cs - re * sn], axis=1))
        parts = split_n(jnp.concatenate(turned, axis=0), pieces)
        out = sum(mm(parts[n], T["qf"][k], NN) for n in range(pieces) for k in range(pieces - n))
        return [(out[128 * ii : 128 * ii + 128, :128], out[128 * ii : 128 * ii + 128, 128:]) for ii in range(four)]

    def x_part(i):
        g, e = me // 16, me % 16
        t = e + 16 * i
        lane = lax.broadcasted_iota(jnp.int32, (1, 128), 1)
        k2 = 2 * g + lane // 64
        j2 = jnp.where(t % 2 == 1, -((t + 1) // 2), t // 2)
        kx = jnp.where(k2 == 0, 16 * t, k2 + 32 * j2)
        kappa_x = factor * kx.astype(f32)
        weight = jnp.where(kx == 0, 1.0, 2.0) / (float(N) * float(N))
        return kappa_x, (jnp.abs(kx) <= CUT).astype(f32), weight

    for m in range(3):
        arrive(s1, r1, m, m, 8 if m < 2 else 6)
        four = forward_four(r1, m, 3)
        for ii in range(len(four)):
            vort_ref[4 * m + ii, :, :128], vort_ref[4 * m + ii, :, 128:] = four[ii]

        def slot(i, _):
            kappa_x, kept_x, weight = x_part(i)
            kept = kept_y * kept_x
            kappa_sq = kappa_x * kappa_x + kappa_y * kappa_y
            vr, vi = vort_ref[i, :, :128] * kept, vort_ref[i, :, 128:] * kept
            vort_ref[i, :, :128], vort_ref[i, :, 128:] = vr, vi
            positive = kappa_sq > 0
            inverse_sq = jnp.where(positive, 1.0 / jnp.where(positive, kappa_sq, 1.0), 0.0)
            sr, si = vr * inverse_sq, vi * inverse_sq
            kxw, kyw = kappa_x * weight, kappa_y * weight
            fields = [
                jnp.concatenate([-kyw * si, kyw * sr], axis=1),
                jnp.concatenate([kxw * si, -kxw * sr], axis=1),
                jnp.concatenate([-kxw * vi, kxw * vr], axis=1),
                jnp.concatenate([-kyw * vi, kyw * vr], axis=1),
            ]
            outs = column_backward(fields, T["tc"], T["bo"], pair(T["qb"]))
            for f in range(4):
                for ri in range(2):
                    s2[i, pl.ds(f * 2 + ri, 128, stride=8), :] = outs[f][128 * ri : 128 * ri + 128]
            send(s2, r2, i, 3 + i)
            return 0

        lax.fori_loop(4 * m, min(4 * m + 4, 11), slot, 0)

    def gather_rows(f, g, slots):
        parts = []
        for ri in range(2):
            for i in slots:
                parts.append(r2[i, pl.ds(g * 128 + f * 2 + ri, 16, stride=8), :])
        return split(jnp.concatenate(parts, axis=0))

    def three(a, th, tl):
        return mm(a[0], th, NN) + (mm(a[0], tl, NN) + mm(a[1], th, NN))

    for part, (slots, table) in enumerate(((range(8), "g8"), (range(8, 11), "g3"))):
        for i in slots:
            arrive(s2, r2, i, 3 + i)
        gt = T[table]

        def value(fgs, kind, rows):
            got = [gather_rows(f, g, slots) for f, g in fgs]
            if part == 0:
                both = [jnp.concatenate([a[j].T[:rows] for a in got], axis=0) for j in range(2)]
                return three(both, gt[0, kind], gt[1, kind])
            both = [jnp.concatenate([a[0], a[0], a[1]], axis=0).T[:rows] for a in got]
            return mm(jnp.concatenate(both, axis=0), gt[kind], NN)

        def pairs(n, _):
            f, step = n // 2, n % 2
            out = value([(f, 4 * step + k) for k in range(4)], 0, 128)
            to = pl.ds(pl.multiple_of(step * 512, 512), 512)
            u4[f, to, :] = out if part == 0 else u4[f, to, :] + out
            return 0

        lax.fori_loop(0, 8, pairs, 0)

        edge = value([(f, 0) for f in range(4)], 1, 64)
        for f in range(4):
            out = edge[64 * f : 64 * f + 64]
            up[f] = out if part == 0 else up[f] + out

    def grid_values(u, edge, tw, step, lanes, ims, stride):
        ends = (edge[rows8(step), lanes], edge[rows8(step), ims])
        rest = [None] * 16
        for k in range(1, 16):
            cs, sn = tw[0, k : k + 1, lanes], tw[1, k : k + 1, lanes]
            at = rows8(k * stride + step)
            r, i = u[at, lanes], u[at, ims]
            rest[k] = (r * cs - i * sn, r * sn + i * cs)
        return backward32(ends, rest)

    def radix_product(step, _):
        row = lax.broadcasted_iota(jnp.int32, (8, 128), 0) + (me * 64 + step * 8)
        drive = forcing * jnp.sin((2.0 * math.pi * force_waves / N) * row.astype(f32))
        for h in range(2):
            lanes, ims = pl.ds(128 * h, 128), pl.ds(256 + 128 * h, 128)
            vals = [None] * 4
            for f in (0, 2, 1, 3):
                vals[f] = grid_values(u4.at[f], up.at[f], T["tw"], step, lanes, ims, 8)
                if f == 2:
                    total = [vals[0][q] * vals[2][q] for q in range(32)]
            x = [total[q] + vals[1][q] * vals[3][q] - drive for q in range(32)]
            put_forward(step, x, lanes, h, rows8(step))
        return 0

    lax.fori_loop(0, 8, radix_product, 0)
    row_products(s3, r3, 14, 2, lambda: None)

    inside_one = jnp.concatenate([(jnp.abs(ky) < 2048).astype(f32)] * 2, axis=1)
    inside_two = jnp.concatenate([(jnp.abs(ky) < 1024).astype(f32)] * 2, axis=1)

    def whole_blocks(m, blocks):
        outs = column_backward(blocks, T["tc"], T["bo"], pair(T["qb"]))
        for ii, out in enumerate(outs):
            for ri in range(2):
                to, r = (m, ri * 4 + ii) if m < 2 else (3, ri * 3 + ii)
                s4[to, pl.ds(r, 128, stride=8), :] = out[128 * ri : 128 * ri + 128]

    for m in range(3):
        arrive(s3, r3, m, 14 + m, 8 if m < 2 else 6)
        blocks = []
        for ii, (ar, ai) in enumerate(forward_four(r3, m, 2)):
            i = 4 * m + ii
            kappa_x, kept_x, weight = x_part(i)
            kept = kept_y * kept_x
            kappa_sq = kappa_x * kappa_x + kappa_y * kappa_y
            vr, vi = vort_ref[i, :, :128], vort_ref[i, :, 128:]
            ar, ai = ar * kept, ai * kept
            nr = (vr + half_step * (-ar - viscosity * kappa_sq * vr)) * weight
            ni = (vi + half_step * (-ai - viscosity * kappa_sq * vi)) * weight
            blocks.append(jnp.concatenate([nr, ni], axis=1))
            if i < 8:
                next_ref[i] = blocks[-1]
        if m == 0:
            whole_blocks(0, blocks)
            send(s4, r4, 0, 17)
        if m == 1:
            pairs_of = [
                jnp.concatenate([next_ref[2 * n] * inside_one, next_ref[2 * n + 1] * inside_one], axis=1)
                for n in range(4)
            ]
            for n, out in enumerate(column_backward(pairs_of, T["tc1"], T["bo"], pair(T["q1"]))):
                for ri in range(2):
                    s4[2, pl.ds(2 * n + ri, 128, stride=8), :] = out[128 * ri : 128 * ri + 128]
            send(s4, r4, 2, 19)
            block = jnp.concatenate([next_ref[n] * inside_two for n in range(4)], axis=1)
            (out,) = column_backward([block], T["tc2"], T["bo"], pair(T["q2"]))
            for ri in range(2):
                s4[4, pl.ds(ri, 128, stride=8), :] = out[128 * ri : 128 * ri + 128]
            send(s4, r4, 4, 21, 2)
            whole_blocks(1, blocks)
            send(s4, r4, 1, 18)
        if m == 2:
            whole_blocks(2, blocks)
            send(s4, r4, 3, 20, 6)

    def transposed(m, g, valid=8):
        block = r4[m, pl.ds(pl.multiple_of(g * 128, 128), 128), :]
        if valid < 8:
            row = lax.broadcasted_iota(jnp.int32, (128, 128), 0) % 8
            block = jnp.where(row < valid, block, 0.0)
        high, low = split(block)
        return high.T, low.T

    def coarse(m, table, u, each, valid):
        copies = 64 // each

        def value(gs, kind):
            both = [[], []]
            for g in gs:
                a = transposed(m, g, valid)
                for j in range(2):
                    parts = [a[j][n * 2 * each : (n + 1) * 2 * each] for n in range(copies)]
                    both[j].append(jnp.concatenate(parts, axis=1))
            both = [jnp.concatenate(v, axis=0) for v in both]
            return three(both, table[0, kind], table[1, kind])

        def product(n, _):
            out = value([4 * n + k for k in range(4)], 0)
            u[pl.ds(pl.multiple_of(n * 8 * each, 8 * each), 8 * each), :] = out
            return 0

        lax.fori_loop(0, 2, product, 0)
        u[:each, :] = value([0], 1)[:each]

    right, left = (sub + 1) % 4, (sub + 3) % 4

    def ring(value, out, each, base):
        def rows(owner, start, size):
            return out.at[pl.ds(pl.multiple_of(owner * each + start, 8), size)]

        def remote(src, dst, to, sem):
            return pltpu.make_async_remote_copy(
                src_ref=src,
                dst_ref=dst,
                send_sem=gather_send.at[base + sem],
                recv_sem=gather_recv.at[base + sem],
                device_id=(band, to),
                device_id_type=MESH,
            )

        mine = rows(sub, 0, each)
        own = pltpu.make_async_copy(value, mine, out_sem.at[base // 4])
        first = [remote(value, mine, right, 0), remote(value, mine, left, 1)]
        half = each // 2
        a, b = rows(left, 0, half), rows(right, half, half)
        second = [remote(a, a, right, 2), remote(b, b, left, 3)]

        def start():
            own.start()
            for copy in first:
                copy.start()

        def forward():
            for n in range(2):
                first[n].wait_recv()
                second[n].start()

        def finish():
            own.wait()
            for copy in first:
                copy.wait_send()
            for copy in second:
                copy.wait_send()
                copy.wait_recv()

        return start, forward, finish

    ring_one, ring_two = ring(one_v, one_ref, 32, 0), ring(two_v, two_ref, 16, 4)

    arrive(s4, r4, 2, 19)
    coarse(2, T["c1"], u1, 32, 8)

    def radix_one(step, _):
        out = grid_values(u1, u1, T["tw1"], step, pl.ds(0, 128), pl.ds(128, 128), 4)
        for q in range(32):
            one_v[rows8(step), pl.ds(128 * q, 128)] = out[q]
        return 0

    lax.fori_loop(0, 4, radix_one, 0)
    ring_one[0]()

    arrive(s4, r4, 4, 21, 2)
    coarse(4, T["c2"], u2, 16, 2)

    def radix_two(step, _):
        out = grid_values(u2, u2, T["tw2"], step, pl.ds(0, 64), pl.ds(64, 64), 2)
        for q in range(16):
            two_v[rows8(step), pl.ds(128 * q, 128)] = jnp.concatenate([out[2 * q], out[2 * q + 1]], axis=1)
        return 0

    lax.fori_loop(0, 2, radix_two, 0)
    ring_two[0]()

    arrive(s4, r4, 0, 17)
    arrive(s4, r4, 1, 18)
    u0, u0p = u4.at[0], up.at[0]

    def section_first(step, _):
        parts = [[transposed(m, 4 * step + g) for m in range(2)] for g in range(4)]
        both = [
            jnp.concatenate([jnp.concatenate([parts[g][0][j], parts[g][1][j]], axis=1) for g in range(4)], axis=0)
            for j in range(2)
        ]
        u0[pl.ds(pl.multiple_of(step * 512, 512), 512), :] = three(both, T["e8"][0, 0], T["e8"][1, 0])
        return 0

    lax.fori_loop(0, 2, section_first, 0)
    parts = [transposed(m, 0) for m in range(2)]
    both = [jnp.concatenate([parts[0][j][:64], parts[1][j][:64]], axis=1) for j in range(2)]
    u0p[...] = three(both, T["e8"][0, 1], T["e8"][1, 1])
    ring_one[1]()
    ring_two[1]()

    arrive(s4, r4, 3, 20, 6)

    def section_last(step, _):
        a = [transposed(3, 4 * step + g, 6) for g in range(4)]
        both = [jnp.concatenate([v[j] for v in a], axis=0) for j in range(2)]
        to = pl.ds(pl.multiple_of(step * 512, 512), 512)
        u0[to, :] = u0[to, :] + three(both, T["e3"][0, 0], T["e3"][1, 0])
        return 0

    lax.fori_loop(0, 2, section_last, 0)
    a = transposed(3, 0, 6)
    u0p[...] = u0p[...] + three((a[0][:64], a[1][:64]), T["e3"][0, 1], T["e3"][1, 1])

    def radix_section(step, _):
        for h in range(2):
            lanes, ims = pl.ds(128 * h, 128), pl.ds(256 + 128 * h, 128)
            out = grid_values(u0, u0p, T["tw"], step, lanes, ims, 8)
            for q in range(32):
                x_v[rows8(step), pl.ds(256 * q + 128 * h, 128)] = out[q]
        return 0

    lax.fori_loop(0, 8, radix_section, 0)
    final = pltpu.make_async_copy(x_v, section_ref, out_sem.at[2])
    final.start()
    for m in range(3):
        whole(s1, r1, m, m, 8 if m < 2 else 6).wait_send()
        whole(s3, r3, m, 14 + m, 8 if m < 2 else 6).wait_send()
    for i in range(11):
        whole(s2, r2, i, 3 + i).wait_send()
    for m, each in enumerate((8, 8, 8, 6, 2)):
        whole(s4, r4, m, 17 + m, each).wait_send()
    ring_one[2]()
    ring_two[2]()
    final.wait()


def split_n(x, pieces):
    out = []
    for _ in range(pieces):
        out.append(x.astype(bf16))
        x = x - out[-1].astype(f32)
    return out


def wave_y():
    k = lax.broadcasted_iota(jnp.int32, (128, 128), 0)
    lane = lax.broadcasted_iota(jnp.int32, (128, 128), 1)
    j = lane % 64
    return k + 128 * jnp.where(j < 32, j, j - 64)


def column_backward(fields, tc_ref, bo_ref, qb_table):
    stacked = jnp.concatenate(fields, axis=0) if len(fields) > 1 else fields[0]
    u = dot_right(stacked, qb_table)
    c, s = tc_ref[0], tc_ref[1]
    cols = []
    for n in range(len(fields)):
        r, im = u[128 * n : 128 * n + 128, :128], u[128 * n : 128 * n + 128, 128:]
        cols.append(jnp.concatenate([r * c - im * s, r * s + im * c], axis=0))
    joined = jnp.concatenate(cols, axis=1) if len(cols) > 1 else cols[0]
    out = dot_left(pair(bo_ref), joined)
    return [out[:, 128 * n : 128 * n + 128] for n in range(len(fields))]


def all_tables():
    fg, fs = forward_row_tables()
    g8, g3 = backward_field_tables()
    e8, e3, c1, c2 = backward_next_tables()
    outer = column_outer()
    inner = column_inner(64, 1, 1)
    return {
        "tw": row_twiddle(N),
        "fg": fg,
        "fs": fs,
        "fo": thirds(outer[0]),
        "tc": column_twiddle(64, 2),
        "qf": thirds(inner.T),
        "bo": halves(outer[1]),
        "qb": halves(inner),
        "g8": g8,
        "g3": g3,
        "tc1": column_twiddle(32, 4),
        "tc2": column_twiddle(16, 8),
        "q1": halves(column_inner(32, 2, 1)),
        "q2": halves(column_inner(16, 4, 1)),
        "e8": e8,
        "e3": e3,
        "c1": c1,
        "c2": c2,
        "tw1": row_twiddle(N // 2),
        "tw2": row_twiddle(N // 4),
    }


def local(vorticity):
    tables = all_tables()
    names = tuple(tables)
    anywhere = pl.BlockSpec(memory_space=pl.ANY)
    shapes = [(64, N), (128, N // 2), (64, N // 4)]
    part = lambda n: (n, 8 * DEV, 128)
    scratch = [(64, N), (1024, 512), part(3), part(3), part(11), part(11), (4, 1024, 512), (4, 64, 512)]
    scratch += [part(3), part(3), part(5), part(5), (12, 128, 256), (8, 128, 256)]
    scratch += [(32, N // 2), (16, N // 4), (512, 256), (256, 128)]
    dma = pltpu.SemaphoreType.DMA
    section, one, two = pl.pallas_call(
        functools.partial(kernel, names),
        out_shape=[jax.ShapeDtypeStruct(s, f32) for s in shapes],
        in_specs=[anywhere] * (1 + len(names)),
        out_specs=[anywhere] * 3,
        scratch_shapes=[pltpu.VMEM(s, f32) for s in scratch]
        + [pltpu.VMEM(t.shape, t.dtype) for t in tables.values()]
        + [dma((22,)), dma((22,)), dma((22,)), dma((len(names) + 1,)), dma((8,)), dma((8,)), dma((3,))],
        compiler_params=pltpu.CompilerParams(
            collective_id=0, has_side_effects=True, vmem_limit_bytes=60 * 2**20
        ),
    )(vorticity, *[jnp.asarray(t) for t in tables.values()])
    return section, one, two


def solution(mesh):
    return jax.shard_map(
        local,
        mesh=mesh,
        in_specs=(P(AXES, None),),
        out_specs=(P(AXES, None), P("band", None), P("band", None)),
        check_vma=False,
    )
```
